32 devices in a mesh: section: 4 (over y, x), strip: 8 (over z, core).
Axes of the slice: x: 2, y: 2, z: 4, core: 2. Of those that a mesh axis runs over, the one named last changes fastest.
Arguments:
- images: bfloat16 [2, 32, 32, 256], P(None, 'strip'), may hold values from -6 to 6
- conv_first: bfloat16 [4, 9, 256, 256], P('section'), may hold values from -0.1875 to 0.1875
- conv_skip: bfloat16 [4, 9, 256, 256], P('section'), may hold values from -0.09375 to 0.09375
- conv_second: bfloat16 [4, 9, 256, 256], P('section'), may hold values from -0.1875 to 0.1875
- bias_first: float32 [4, 256], P('section'), may hold values from -0.8 to 0.8
- bias_second: float32 [4, 256], P('section'), may hold values from -0.8 to 0.8
Outputs:
- activations: bfloat16 [4, 2, 32, 32, 256], P('section', None, 'strip')
The draws below stay inside these ranges and needn't reach their ends.
All inputs are finite; a program needn't handle non-finite values.
Results may differ from the reference program's by a relative error of at most 0.02.
Values may be sent and summed in bfloat16 or wider, within the bound.
A program may use at most 64 MiB of HBM per device.

```python
import jax
import jax.numpy as jnp

CHANNELS = 256
COLUMNS = 32
MICRO = 2
SECTIONS = 4
HEIGHT = 32


def level_of(rng, dims, pieces, least, largest):
    loudness, own = 1.0, jax.random.fold_in(rng, 6)
    for position, shards_of in pieces:
        steps = jnp.exp(jax.random.uniform(jax.random.fold_in(own, position), (shards_of,), jnp.float32, least / len(pieces), largest / len(pieces)))
        loudness = loudness * jnp.repeat(steps, dims[position] // shards_of).reshape([-1 if axis == position else 1 for axis in range(len(dims))])
    return loudness


def scatter_about(own_key, shape, deviation, reach, cuts=(), kind=jnp.bfloat16):
    array = deviation * jax.random.normal(own_key, shape, jnp.float32)
    if cuts:
        array = array * level_of(own_key, shape, cuts, -0.22, 0.18)
    return jnp.clip(array, -reach, reach).astype(kind)


def setup_inputs(seed: int = 0) -> dict:
    streams_of = jax.random.split(jax.random.key(seed), 7)
    images = scatter_about(streams_of[0], (MICRO, HEIGHT, COLUMNS, CHANNELS), 1.0, 6.0, ((1, 8),))
    conv_first = scatter_about(streams_of[1], (SECTIONS, 9, CHANNELS, CHANNELS), (9 * CHANNELS // 2) ** -0.5, 0.1875, ((0, 4),))
    conv_skip = scatter_about(streams_of[2], (SECTIONS, 9, CHANNELS, CHANNELS), (18 * CHANNELS) ** -0.5, 0.09375, ((0, 4),))
    conv_second = scatter_about(streams_of[3], (SECTIONS, 9, CHANNELS, CHANNELS), (9 * CHANNELS // 2) ** -0.5, 0.1875, ((0, 4),))
    bias_first = scatter_about(streams_of[4], (SECTIONS, CHANNELS), 0.2, 0.8, ((0, 4),), jnp.float32)
    bias_second = scatter_about(streams_of[5], (SECTIONS, CHANNELS), 0.2, 0.8, ((0, 4),), jnp.float32)
    return {"images": images, "conv_first": conv_first, "conv_skip": conv_skip, "conv_second": conv_second, "bias_first": bias_first, "bias_second": bias_second}


def convolve(feature, weight):
    height_rows = feature.shape[0]
    width_cols = feature.shape[1]
    channels = feature.shape[2]
    padded = jnp.pad(feature, ((1, 1), (1, 1), (0, 0)))
    summed = jnp.zeros((height_rows * width_cols, weight.shape[2]), jnp.float32)
    for tap_index in range(9):
        row_offset = tap_index // 3
        column_offset = tap_index % 3
        window_rows = padded[row_offset:row_offset + height_rows, column_offset:column_offset + width_cols]
        window_rows = window_rows.reshape(height_rows * width_cols, channels)
        summed = summed + jnp.dot(window_rows, weight[tap_index], preferred_element_type=jnp.float32)
    return summed.reshape(height_rows, width_cols, weight.shape[2])


def reference(images, conv_first, conv_skip, conv_second, bias_first, bias_second):
    per_section = [[] for section_index in range(SECTIONS)]
    for micro_index in range(MICRO):
        current = images[micro_index]
        for section_index in range(SECTIONS):
            preact = convolve(current, conv_first[section_index])
            if section_index >= SECTIONS // 2:
                preact = preact + convolve(per_section[SECTIONS - 1 - section_index][micro_index], conv_skip[section_index])
            hidden = jax.nn.relu(preact + bias_first[section_index]).astype(jnp.bfloat16)
            result = jax.nn.relu(convolve(hidden, conv_second[section_index]) + bias_second[section_index]).astype(jnp.bfloat16)
            per_section[section_index].append(result)
            current = result
    return jnp.stack([jnp.stack(section_list) for section_list in per_section])
```

```python
import functools

import jax
import jax.numpy as jnp
from jax import lax
from jax.experimental import pallas as pl
from jax.experimental.pallas import tpu as pltpu
from jax.sharding import PartitionSpec as P

MESH = pl.DeviceIdType.MESH
HALO = 2


def kernel(
    sections, strips,
    images, conv_first, conv_skip, conv_second, bias_first, bias_second,
    out,
    first_w, skip_w, second_w, first_b, second_b,
    land, skip_land, result, pre,
    weight_sem, image_sem, edge_send, land_recv, land_send, skip_recv, skip_send, out_sem,
):
    section = lax.axis_index("section")
    strip = lax.axis_index("strip")
    micro, rows, cols, channels = result.shape
    taps = 9 * channels
    middle = sections // 2
    is_first = section == 0
    has_next = section + 1 < sections
    has_above = strip > 0
    has_below = strip + 1 < strips
    sends_skip = section < middle - 1
    takes_skip = section > middle
    mirror = sections - 1 - section

    weights = (
        pltpu.make_async_copy(conv_first.at[0], first_w, weight_sem.at[0]),
        pltpu.make_async_copy(conv_second.at[0], second_w, weight_sem.at[1]),
        pltpu.make_async_copy(bias_first, first_b, weight_sem.at[2]),
        pltpu.make_async_copy(bias_second, second_b, weight_sem.at[3]),
    )
    skip_weight = pltpu.make_async_copy(conv_skip.at[0], skip_w, weight_sem.at[4])
    own_rows = pltpu.make_async_copy(images, land.at[:, pl.ds(HALO, rows)], image_sem)

    def pieces(source, target, m, to_section, send, recv):
        return (
            (None, pltpu.make_async_remote_copy(
                src_ref=source.at[m], dst_ref=target.at[m, pl.ds(HALO, rows)],
                send_sem=send.at[m, 0], recv_sem=recv.at[m, 0],
                device_id=(to_section, strip), device_id_type=MESH)),
            (has_above, pltpu.make_async_remote_copy(
                src_ref=source.at[m, pl.ds(0, HALO)], dst_ref=target.at[m, pl.ds(HALO + rows, HALO)],
                send_sem=send.at[m, 1], recv_sem=recv.at[m, 1],
                device_id=(to_section, strip - 1), device_id_type=MESH)),
            (has_below, pltpu.make_async_remote_copy(
                src_ref=source.at[m, pl.ds(rows - HALO, HALO)], dst_ref=target.at[m, pl.ds(0, HALO)],
                send_sem=send.at[m, 2], recv_sem=recv.at[m, 2],
                device_id=(to_section, strip + 1), device_id_type=MESH)),
        )

    def onward(m):
        return pieces(result, land, m, section + 1, land_send, land_recv)

    def skipped(m):
        return pieces(result, skip_land, m, mirror, skip_send, skip_recv)

    def edges(m):
        return pieces(images, land, m, section, edge_send, land_recv)[1:]

    def start(group):
        for condition, copy in group:
            if condition is None:
                copy.start()
            else:
                pl.when(condition)(copy.start)

    def wait_sent(group):
        for condition, copy in group:
            if condition is None:
                copy.wait_send()
            else:
                pl.when(condition)(copy.wait_send)

    def wait_arrived(group):
        for condition, copy in group:
            if condition is None:
                copy.wait_recv()
            elif condition is has_above:
                pl.when(has_below)(copy.wait_recv)
            else:
                pl.when(has_above)(copy.wait_recv)

    for copy in weights:
        copy.start()
    pl.when(section >= middle)(skip_weight.start)
    pl.when(is_first)(own_rows.start)

    barrier = pltpu.get_barrier_semaphore()

    def greet(condition, to_section, with_own):
        @pl.when(condition)
        def _():
            if with_own:
                pl.semaphore_signal(barrier, inc=1, device_id=(to_section, strip), device_id_type=MESH)

            @pl.when(has_above)
            def _():
                pl.semaphore_signal(barrier, inc=1, device_id=(to_section, strip - 1), device_id_type=MESH)

            @pl.when(has_below)
            def _():
                pl.semaphore_signal(barrier, inc=1, device_id=(to_section, strip + 1), device_id_type=MESH)

    greet(is_first, section, False)
    greet(section > 0, section - 1, True)
    greet(takes_skip, mirror, True)

    beside = has_above.astype(jnp.int32) + has_below.astype(jnp.int32)
    expected = (
        jnp.where(is_first, beside, 0)
        + jnp.where(has_next, beside + 1, 0)
        + jnp.where(sends_skip, beside + 1, 0)
    )
    @pl.when(expected > 0)
    def _():
        pl.semaphore_wait(barrier, expected)

    @pl.when(is_first)
    def _():
        for m in range(micro):
            start(edges(m))

    blank = jnp.zeros((micro, HALO, cols, channels), land.dtype)

    @pl.when(jnp.logical_not(has_above))
    def _():
        land[:, 0:HALO] = blank
        skip_land[:, 0:HALO] = blank

    @pl.when(jnp.logical_not(has_below))
    def _():
        land[:, HALO + rows:] = blank
        skip_land[:, HALO + rows:] = blank

    pl.when(section >= middle)(skip_weight.wait)
    for copy in weights:
        copy.wait()

    @pl.when(section == middle)
    def _():
        def add(tap, carry):
            total = first_w[tap].astype(jnp.float32) + skip_w[tap].astype(jnp.float32)
            first_w[tap] = total.astype(first_w.dtype)
            return carry
        lax.fori_loop(0, 9, add, 0)

    pl.when(is_first)(own_rows.wait)

    def convolve(value, weight):
        in_rows = value.shape[0] // cols
        out_rows = in_rows - 2
        column = lax.rem(lax.broadcasted_iota(jnp.int32, value.shape, 0), cols)
        size = value.shape[0]
        left = jnp.where(column == 0, 0.0, pltpu.roll(value, 1, axis=0)).astype(jnp.bfloat16)
        centre = value.astype(jnp.bfloat16)
        right = jnp.where(column == cols - 1, 0.0, pltpu.roll(value, size - 1, axis=0)).astype(jnp.bfloat16)
        windows = [
            part[a * cols:(a + out_rows) * cols] for a in range(3) for part in (left, centre, right)
        ]
        return jnp.dot(
            jnp.concatenate(windows, axis=1),
            weight[...].reshape(taps, channels),
            preferred_element_type=jnp.float32,
        )

    def widened(buffer, m):
        return buffer[m].astype(jnp.float32).reshape((rows + 2 * HALO) * cols, channels)

    hidden_rows = rows + 2

    def step(m, carry):
        @pl.when(takes_skip)
        def _():
            wait_arrived(skipped(m))
            pre[...] = convolve(widened(skip_land, m), skip_w) + first_b[...]

        @pl.when(jnp.logical_not(takes_skip))
        def _():
            pre[...] = jnp.broadcast_to(first_b[...], pre.shape)

        @pl.when(is_first)
        def _():
            wait_arrived(edges(m))

        @pl.when(section > 0)
        def _():
            wait_arrived(onward(m))

        hidden = jnp.maximum(convolve(widened(land, m), first_w) + pre[...], 0.0)
        row = lax.broadcasted_iota(jnp.int32, hidden.shape, 0)
        least = jnp.where(has_above, 0, cols)
        most = jnp.where(has_below, hidden_rows * cols, (hidden_rows - 1) * cols)
        hidden = jnp.where((row >= least) & (row < most), hidden, 0.0)
        final = jnp.maximum(convolve(hidden, second_w) + second_b[...], 0.0)
        result[m] = final.astype(jnp.bfloat16).reshape(rows, cols, channels)

        @pl.when(has_next)
        def _():
            start(onward(m))

        pltpu.make_async_copy(result.at[m], out.at[0, m], out_sem.at[m]).start()
        return carry

    lax.fori_loop(0, micro, step, 0)

    @pl.when(sends_skip)
    def _():
        for m in range(micro):
            start(skipped(m))

    for m in range(micro):
        pltpu.make_async_copy(result.at[m], out.at[0, m], out_sem.at[m]).wait()

        @pl.when(is_first)
        def _():
            wait_sent(edges(m))

        @pl.when(has_next)
        def _():
            wait_sent(onward(m))

        @pl.when(sends_skip)
        def _():
            wait_sent(skipped(m))


def body(images, conv_first, conv_skip, conv_second, bias_first, bias_second):
    sections = lax.axis_size("section")
    strips = lax.axis_size("strip")
    micro, rows, cols, channels = images.shape
    padded = (micro, rows + 2 * HALO, cols, channels)
    weight = conv_first.shape[1:]
    copies = pltpu.SemaphoreType.DMA((micro, 3))
    pixels = rows * cols
    flops = 2 * micro * 2 * pixels * channels * channels * 9
    return pl.pallas_call(
        functools.partial(kernel, sections, strips),
        out_shape=jax.ShapeDtypeStruct((1, micro, rows, cols, channels), jnp.bfloat16),
        in_specs=[pl.BlockSpec(memory_space=pl.ANY)] * 6,
        out_specs=pl.BlockSpec(memory_space=pl.ANY),
        scratch_shapes=[
            pltpu.VMEM(weight, jnp.bfloat16),
            pltpu.VMEM(weight, jnp.bfloat16),
            pltpu.VMEM(weight, jnp.bfloat16),
            pltpu.VMEM((1, channels), jnp.float32),
            pltpu.VMEM((1, channels), jnp.float32),
            pltpu.VMEM(padded, jnp.bfloat16),
            pltpu.VMEM(padded, jnp.bfloat16),
            pltpu.VMEM((micro, rows, cols, channels), jnp.bfloat16),
            pltpu.VMEM(((rows + 2) * cols, channels), jnp.float32),
            pltpu.SemaphoreType.DMA((5,)),
            pltpu.SemaphoreType.DMA,
            copies, copies, copies, copies, copies,
            pltpu.SemaphoreType.DMA((micro,)),
        ],
        compiler_params=pltpu.CompilerParams(
            collective_id=0, has_side_effects=True, vmem_limit_bytes=32 * 1024 * 1024
        ),
        cost_estimate=pl.CostEstimate(
            flops=flops, bytes_accessed=3 * conv_first.size * 2, transcendentals=0
        ),
    )(images, conv_first, conv_skip, conv_second, bias_first, bias_second)


def solution(mesh):
    placed = (
        P(None, "strip", None, None),
        P("section", None, None, None),
        P("section", None, None, None),
        P("section", None, None, None),
        P("section", None),
        P("section", None),
    )
    return jax.shard_map(
        body,
        mesh=mesh,
        in_specs=placed,
        out_specs=P("section", None, "strip", None, None),
        check_vma=False,
    )
```

```python
import functools

import jax
import jax.numpy as jnp
from jax import lax
from jax.experimental import pallas as pl
from jax.experimental.pallas import tpu as pltpu
from jax.sharding import PartitionSpec as P

MESH = pl.DeviceIdType.MESH
HALO = 2


def kernel(
    sections, strips,
    images, conv_first, conv_skip, conv_second, bias_first, bias_second,
    out,
    first_w, skip_w, second_w, first_b, second_b,
    land, skip_land, result, pre,
    weight_sem, image_sem, edge_send, land_recv, land_send, skip_recv, skip_send, out_sem,
):
    section = lax.axis_index("section")
    strip = lax.axis_index("strip")
    micro, rows, cols, channels = result.shape
    taps = 9 * channels
    middle = sections // 2
    is_first = section == 0
    has_next = section + 1 < sections
    has_above = strip > 0
    has_below = strip + 1 < strips
    sends_skip = (section > 0) & (section < middle)
    takes_skip = section > middle
    mirror = sections - section

    weights = (
        pltpu.make_async_copy(conv_first.at[0], first_w, weight_sem.at[0]),
        pltpu.make_async_copy(conv_second.at[0], second_w, weight_sem.at[1]),
        pltpu.make_async_copy(bias_first, first_b, weight_sem.at[2]),
        pltpu.make_async_copy(bias_second, second_b, weight_sem.at[3]),
    )
    skip_weight = pltpu.make_async_copy(conv_skip.at[0], skip_w, weight_sem.at[4])
    own_rows = pltpu.make_async_copy(images, land.at[:, pl.ds(HALO, rows)], image_sem)

    def pieces(source, target, m, to_section, send, recv):
        return (
            (None, pltpu.make_async_remote_copy(
                src_ref=source.at[m], dst_ref=target.at[m, pl.ds(HALO, rows)],
                send_sem=send.at[m, 0], recv_sem=recv.at[m, 0],
                device_id=(to_section, strip), device_id_type=MESH)),
            (has_above, pltpu.make_async_remote_copy(
                src_ref=source.at[m, pl.ds(0, HALO)], dst_ref=target.at[m, pl.ds(HALO + rows, HALO)],
                send_sem=send.at[m, 1], recv_sem=recv.at[m, 1],
                device_id=(to_section, strip - 1), device_id_type=MESH)),
            (has_below, pltpu.make_async_remote_copy(
                src_ref=source.at[m, pl.ds(rows - HALO, HALO)], dst_ref=target.at[m, pl.ds(0, HALO)],
                send_sem=send.at[m, 2], recv_sem=recv.at[m, 2],
                device_id=(to_section, strip + 1), device_id_type=MESH)),
        )

    def onward(m):
        return pieces(result, land, m, section + 1, land_send, land_recv)

    def skipped(m):
        return pltpu.make_async_remote_copy(
            src_ref=land.at[m], dst_ref=skip_land.at[m],
            send_sem=skip_send.at[m], recv_sem=skip_recv.at[m],
            device_id=(mirror, strip), device_id_type=MESH)

    def edges(m):
        return pieces(images, land, m, section, edge_send, land_recv)[1:]

    def start(group):
        for condition, copy in group:
            if condition is None:
                copy.start()
            else:
                pl.when(condition)(copy.start)

    def wait_sent(group):
        for condition, copy in group:
            if condition is None:
                copy.wait_send()
            else:
                pl.when(condition)(copy.wait_send)

    def wait_arrived(group):
        for condition, copy in group:
            if condition is None:
                copy.wait_recv()
            elif condition is has_above:
                pl.when(has_below)(copy.wait_recv)
            else:
                pl.when(has_above)(copy.wait_recv)

    for copy in weights:
        copy.start()
    pl.when(section >= middle)(skip_weight.start)
    pl.when(is_first)(own_rows.start)

    barrier = pltpu.get_barrier_semaphore()

    def greet_own(condition, to_section):
        @pl.when(condition)
        def _():
            pl.semaphore_signal(barrier, inc=1, device_id=(to_section, strip), device_id_type=MESH)

    def greet_beside(condition, to_section):
        @pl.when(condition)
        def _():
            @pl.when(has_above)
            def _():
                pl.semaphore_signal(barrier, inc=1, device_id=(to_section, strip - 1), device_id_type=MESH)

            @pl.when(has_below)
            def _():
                pl.semaphore_signal(barrier, inc=1, device_id=(to_section, strip + 1), device_id_type=MESH)

    greet_beside(is_first, section)
    greet_own(section > 0, section - 1)
    greet_beside(section > 0, section - 1)
    greet_own(takes_skip, mirror)

    beside = has_above.astype(jnp.int32) + has_below.astype(jnp.int32)
    expected = (
        jnp.where(is_first, beside, 0)
        + jnp.where(has_next, beside + 1, 0)
        + jnp.where(sends_skip, 1, 0)
    )
    @pl.when(expected > 0)
    def _():
        pl.semaphore_wait(barrier, expected)

    @pl.when(is_first)
    def _():
        for m in range(micro):
            start(edges(m))

    blank = jnp.zeros((micro, HALO, cols, channels), land.dtype)

    @pl.when(jnp.logical_not(has_above))
    def _():
        land[:, 0:HALO] = blank

    @pl.when(jnp.logical_not(has_below))
    def _():
        land[:, HALO + rows:] = blank

    pl.when(section >= middle)(skip_weight.wait)
    for copy in weights:
        copy.wait()

    @pl.when(section == middle)
    def _():
        def add(tap, carry):
            total = first_w[tap].astype(jnp.float32) + skip_w[tap].astype(jnp.float32)
            first_w[tap] = total.astype(first_w.dtype)
            return carry
        lax.fori_loop(0, 9, add, 0)

    pl.when(is_first)(own_rows.wait)

    def convolve(value, weight):
        in_rows = value.shape[0] // cols
        out_rows = in_rows - 2
        column = lax.rem(lax.broadcasted_iota(jnp.int32, value.shape, 0), cols)
        size = value.shape[0]
        left = jnp.where(column == 0, 0.0, pltpu.roll(value, 1, axis=0)).astype(jnp.bfloat16)
        centre = value.astype(jnp.bfloat16)
        right = jnp.where(column == cols - 1, 0.0, pltpu.roll(value, size - 1, axis=0)).astype(jnp.bfloat16)
        windows = [
            part[a * cols:(a + out_rows) * cols] for a in range(3) for part in (left, centre, right)
        ]
        return jnp.dot(
            jnp.concatenate(windows, axis=1),
            weight[...].reshape(taps, channels),
            preferred_element_type=jnp.float32,
        )

    def widened(buffer, m):
        return buffer[m].astype(jnp.float32).reshape((rows + 2 * HALO) * cols, channels)

    hidden_rows = rows + 2

    def step(m, carry):
        @pl.when(takes_skip)
        def _():
            skipped(m).wait_recv()
            pre[...] = convolve(widened(skip_land, m), skip_w) + first_b[...]

        @pl.when(jnp.logical_not(takes_skip))
        def _():
            pre[...] = jnp.broadcast_to(first_b[...], pre.shape)

        @pl.when(is_first)
        def _():
            wait_arrived(edges(m))

        @pl.when(section > 0)
        def _():
            wait_arrived(onward(m))

        hidden = jnp.maximum(convolve(widened(land, m), first_w) + pre[...], 0.0)
        row = lax.broadcasted_iota(jnp.int32, hidden.shape, 0)
        least = jnp.where(has_above, 0, cols)
        most = jnp.where(has_below, hidden_rows * cols, (hidden_rows - 1) * cols)
        hidden = jnp.where((row >= least) & (row < most), hidden, 0.0)
        final = jnp.maximum(convolve(hidden, second_w) + second_b[...], 0.0)
        result[m] = final.astype(jnp.bfloat16).reshape(rows, cols, channels)

        @pl.when(has_next)
        def _():
            start(onward(m))

        @pl.when(sends_skip)
        def _():
            skipped(m).start()

        pltpu.make_async_copy(result.at[m], out.at[0, m], out_sem.at[m]).start()
        return carry

    lax.fori_loop(0, micro, step, 0)

    for m in range(micro):
        pltpu.make_async_copy(result.at[m], out.at[0, m], out_sem.at[m]).wait()

        @pl.when(is_first)
        def _():
            wait_sent(edges(m))

        @pl.when(has_next)
        def _():
            wait_sent(onward(m))

        @pl.when(sends_skip)
        def _():
            skipped(m).wait_send()


def body(images, conv_first, conv_skip, conv_second, bias_first, bias_second):
    sections = lax.axis_size("section")
    strips = lax.axis_size("strip")
    micro, rows, cols, channels = images.shape
    padded = (micro, rows + 2 * HALO, cols, channels)
    weight = conv_first.shape[1:]
    copies = pltpu.SemaphoreType.DMA((micro, 3))
    pixels = rows * cols
    flops = 2 * micro * 2 * pixels * channels * channels * 9
    return pl.pallas_call(
        functools.partial(kernel, sections, strips),
        out_shape=jax.ShapeDtypeStruct((1, micro, rows, cols, channels), jnp.bfloat16),
        in_specs=[pl.BlockSpec(memory_space=pltpu.HBM)] * 6,
        out_specs=pl.BlockSpec(memory_space=pltpu.HBM),
        scratch_shapes=[
            pltpu.VMEM(weight, jnp.bfloat16),
            pltpu.VMEM(weight, jnp.bfloat16),
            pltpu.VMEM(weight, jnp.bfloat16),
            pltpu.VMEM((1, channels), jnp.float32),
            pltpu.VMEM((1, channels), jnp.float32),
            pltpu.VMEM(padded, jnp.bfloat16),
            pltpu.VMEM(padded, jnp.bfloat16),
            pltpu.VMEM((micro, rows, cols, channels), jnp.bfloat16),
            pltpu.VMEM(((rows + 2) * cols, channels), jnp.float32),
            pltpu.SemaphoreType.DMA((5,)),
            pltpu.SemaphoreType.DMA,
            copies, copies, copies,
            pltpu.SemaphoreType.DMA((micro,)),
            pltpu.SemaphoreType.DMA((micro,)),
            pltpu.SemaphoreType.DMA((micro,)),
        ],
        compiler_params=pltpu.CompilerParams(
            collective_id=0, has_side_effects=True, vmem_limit_bytes=32 * 1024 * 1024
        ),
        cost_estimate=pl.CostEstimate(
            flops=flops, bytes_accessed=3 * conv_first.size * 2, transcendentals=0
        ),
    )(images, conv_first, conv_skip, conv_second, bias_first, bias_second)


def solution(mesh):
    placed = (
        P(None, "strip", None, None),
        P("section", None, None, None),
        P("section", None, None, None),
        P("section", None, None, None),
        P("section", None),
        P("section", None),
    )
    return jax.shard_map(
        body,
        mesh=mesh,
        in_specs=placed,
        out_specs=P("section", None, "strip", None, None),
        check_vma=False,
    )
```

```python
import functools

import jax
import jax.numpy as jnp
from jax import lax
from jax.experimental import pallas as pl
from jax.experimental.pallas import tpu as pltpu
from jax.sharding import PartitionSpec as P

MESH = pl.DeviceIdType.MESH
HALO = 2


def kernel(
    sections, strips,
    images, conv_first, conv_skip, conv_second, bias_first, bias_second,
    out,
    first_w, skip_w, second_w, first_b, second_b,
    land, skip_land, result, pre,
    weight_sem, image_sem, edge_send, edge_recv, land_send, land_recv, skip_send, skip_recv, out_sem,
):
    section = lax.axis_index("section")
    strip = lax.axis_index("strip")
    micro, rows, cols, channels = result.shape
    taps = 9 * channels
    middle = sections // 2
    is_first = section == 0
    has_next = section + 1 < sections
    has_above = strip > 0
    has_below = strip + 1 < strips
    sends_skip = (section > 0) & (section < middle)
    takes_skip = section > middle
    mirror = sections - section

    weights = (
        pltpu.make_async_copy(conv_first.at[0], first_w, weight_sem.at[0]),
        pltpu.make_async_copy(conv_second.at[0], second_w, weight_sem.at[1]),
        pltpu.make_async_copy(bias_first, first_b, weight_sem.at[2]),
        pltpu.make_async_copy(bias_second, second_b, weight_sem.at[3]),
    )
    skip_weight = pltpu.make_async_copy(conv_skip.at[0], skip_w, weight_sem.at[4])
    own_rows = pltpu.make_async_copy(images, land.at[:, pl.ds(HALO, rows)], image_sem)

    inner_below = lax.rem(strip, 2) == 0
    half = rows // 2
    outer_row = jnp.where(inner_below, 0, rows - half)
    inner_row = jnp.where(inner_below, rows - half, 0)

    def onward(m, part):
        row = (outer_row, inner_row)[part]
        return pltpu.make_async_remote_copy(
            src_ref=result.at[m, pl.ds(row, half)], dst_ref=land.at[m, pl.ds(HALO + row, half)],
            send_sem=land_send.at[m, part], recv_sem=land_recv.at[m, part],
            device_id=(section + 1, strip), device_id_type=MESH)

    def skipped(m):
        return pltpu.make_async_remote_copy(
            src_ref=land.at[m], dst_ref=skip_land.at[m],
            send_sem=skip_send.at[m], recv_sem=skip_recv.at[m],
            device_id=(mirror, strip), device_id_type=MESH)

    def upward(m):
        return pltpu.make_async_remote_copy(
            src_ref=land.at[m, pl.ds(HALO, HALO)], dst_ref=land.at[m, pl.ds(HALO + rows, HALO)],
            send_sem=edge_send.at[m, 0], recv_sem=edge_recv.at[m, 0],
            device_id=(section, strip - 1), device_id_type=MESH)

    def downward(m):
        return pltpu.make_async_remote_copy(
            src_ref=land.at[m, pl.ds(rows, HALO)], dst_ref=land.at[m, pl.ds(0, HALO)],
            send_sem=edge_send.at[m, 1], recv_sem=edge_recv.at[m, 1],
            device_id=(section, strip + 1), device_id_type=MESH)

    def pass_on(m, to_above, to_below):
        @pl.when(has_above & to_above)
        def _():
            upward(m).start()

        @pl.when(has_below & to_below)
        def _():
            downward(m).start()

    for copy in weights:
        copy.start()
    pl.when(section >= middle)(skip_weight.start)
    pl.when(is_first)(own_rows.start)

    barrier = pltpu.get_barrier_semaphore()

    def greet(condition, to_section, to_strip):
        @pl.when(condition)
        def _():
            pl.semaphore_signal(barrier, inc=1, device_id=(to_section, to_strip), device_id_type=MESH)

    greet(has_above, section, strip - 1)
    greet(has_below, section, strip + 1)
    greet(section > 0, section - 1, strip)
    greet(takes_skip, mirror, strip)
    expected = sum(
        condition.astype(jnp.int32) for condition in (has_above, has_below, has_next, sends_skip)
    )

    @pl.when(expected > 0)
    def _():
        pl.semaphore_wait(barrier, expected)

    @pl.when(is_first)
    def _():
        own_rows.wait()
        for m in range(micro):
            pass_on(m, True, True)

    blank = jnp.zeros((micro, HALO, cols, channels), land.dtype)

    @pl.when(jnp.logical_not(has_above))
    def _():
        land[:, 0:HALO] = blank

    @pl.when(jnp.logical_not(has_below))
    def _():
        land[:, HALO + rows:] = blank

    pl.when(section >= middle)(skip_weight.wait)
    for copy in weights:
        copy.wait()

    @pl.when(section == middle)
    def _():
        def add(tap, carry):
            total = first_w[tap].astype(jnp.float32) + skip_w[tap].astype(jnp.float32)
            first_w[tap] = total.astype(first_w.dtype)
            return carry
        lax.fori_loop(0, 9, add, 0)

    def convolve(value, weight):
        in_rows = value.shape[0]
        flat = value.reshape(in_rows * cols, channels)
        column = lax.broadcasted_iota(jnp.int32, value.shape, 1)

        def moved(distance, edge):
            rolled = pltpu.roll(flat, distance % (in_rows * cols), axis=0).reshape(value.shape)
            return jnp.where(column == edge, 0.0, rolled).astype(jnp.bfloat16)

        parts = (moved(1, 0), value.astype(jnp.bfloat16), moved(-1, cols - 1))
        windows = [
            part[a:a + in_rows - 2].reshape((in_rows - 2) * cols, channels)
            for a in range(3) for part in parts
        ]
        return jnp.dot(
            jnp.concatenate(windows, axis=1),
            weight[...].reshape(taps, channels),
            preferred_element_type=jnp.float32,
        )

    def widened(buffer, m):
        return buffer[m].astype(jnp.float32)

    hidden_rows = rows + 2

    def step(m, carry):
        @pl.when(takes_skip)
        def _():
            skipped(m).wait_recv()
            pre[...] = convolve(widened(skip_land, m), skip_w) + first_b[...]

        @pl.when(jnp.logical_not(takes_skip))
        def _():
            pre[...] = jnp.broadcast_to(first_b[...], pre.shape)

        @pl.when(section > 0)
        def _():
            onward(m, 0).wait_recv()
            pass_on(m, inner_below, jnp.logical_not(inner_below))
            onward(m, 1).wait_recv()
            pass_on(m, jnp.logical_not(inner_below), inner_below)

        @pl.when(has_below)
        def _():
            upward(m).wait_recv()

        @pl.when(has_above)
        def _():
            downward(m).wait_recv()

        hidden = jnp.maximum(convolve(widened(land, m), first_w) + pre[...], 0.0)
        hidden = hidden.reshape(hidden_rows, cols, channels)
        row = lax.broadcasted_iota(jnp.int32, hidden.shape, 0)
        least = jnp.where(has_above, 0, 1)
        most = jnp.where(has_below, hidden_rows, hidden_rows - 1)
        hidden = jnp.where((row >= least) & (row < most), hidden, 0.0)
        final = jnp.maximum(convolve(hidden, second_w) + second_b[...], 0.0)
        result[m] = final.astype(jnp.bfloat16).reshape(rows, cols, channels)

        @pl.when(has_next)
        def _():
            onward(m, 0).start()
            onward(m, 1).start()

        @pl.when(sends_skip)
        def _():
            skipped(m).start()

        pltpu.make_async_copy(result.at[m], out.at[0, m], out_sem.at[m]).start()
        return carry

    lax.fori_loop(0, micro, step, 0)

    for m in range(micro):
        pltpu.make_async_copy(result.at[m], out.at[0, m], out_sem.at[m]).wait()

        @pl.when(has_above)
        def _():
            upward(m).wait_send()

        @pl.when(has_below)
        def _():
            downward(m).wait_send()

        @pl.when(has_next)
        def _():
            onward(m, 0).wait_send()
            onward(m, 1).wait_send()

        @pl.when(sends_skip)
        def _():
            skipped(m).wait_send()


def body(images, conv_first, conv_skip, conv_second, bias_first, bias_second):
    sections = lax.axis_size("section")
    strips = lax.axis_size("strip")
    micro, rows, cols, channels = images.shape
    padded = (micro, rows + 2 * HALO, cols, channels)
    weight = conv_first.shape[1:]
    copies = pltpu.SemaphoreType.DMA((micro, 2))
    pixels = rows * cols
    flops = 2 * micro * 2 * pixels * channels * channels * 9
    return pl.pallas_call(
        functools.partial(kernel, sections, strips),
        out_shape=jax.ShapeDtypeStruct((1, micro, rows, cols, channels), jnp.bfloat16),
        in_specs=[pl.BlockSpec(memory_space=pltpu.HBM)] * 6,
        out_specs=pl.BlockSpec(memory_space=pltpu.HBM),
        scratch_shapes=[
            pltpu.VMEM(weight, jnp.bfloat16),
            pltpu.VMEM(weight, jnp.bfloat16),
            pltpu.VMEM(weight, jnp.bfloat16),
            pltpu.VMEM((1, channels), jnp.float32),
            pltpu.VMEM((1, channels), jnp.float32),
            pltpu.VMEM(padded, jnp.bfloat16),
            pltpu.VMEM(padded, jnp.bfloat16),
            pltpu.VMEM((micro, rows, cols, channels), jnp.bfloat16),
            pltpu.VMEM(((rows + 2) * cols, channels), jnp.float32),
            pltpu.SemaphoreType.DMA((5,)),
            pltpu.SemaphoreType.DMA,
            copies, copies, copies, copies,
            pltpu.SemaphoreType.DMA((micro,)),
            pltpu.SemaphoreType.DMA((micro,)),
            pltpu.SemaphoreType.DMA((micro,)),
        ],
        compiler_params=pltpu.CompilerParams(
            collective_id=0, has_side_effects=True
        ),
        cost_estimate=pl.CostEstimate(
            flops=flops, bytes_accessed=3 * conv_first.size * 2, transcendentals=0
        ),
    )(images, conv_first, conv_skip, conv_second, bias_first, bias_second)


def solution(mesh):
    placed = (
        P(None, "strip", None, None),
        P("section", None, None, None),
        P("section", None, None, None),
        P("section", None, None, None),
        P("section", None),
        P("section", None),
    )
    return jax.shard_map(
        body,
        mesh=mesh,
        in_specs=placed,
        out_specs=P("section", None, "strip", None, None),
        check_vma=False,
    )
```

```python
import functools

import jax
import jax.numpy as jnp
from jax import lax
from jax.experimental import pallas as pl
from jax.experimental.pallas import tpu as pltpu
from jax.sharding import PartitionSpec as P

MESH = pl.DeviceIdType.MESH
HALO = 2


def kernel(
    sections, strips,
    images, conv_first, conv_skip, conv_second, bias_first, bias_second,
    out,
    first_w, skip_w, second_w, first_b, second_b,
    land, skip_land, result, hidden_map, pre,
    weight_sem, image_sem, edge_send, edge_recv, skip_edge_send, skip_edge_recv, land_send, land_recv, skip_send, skip_recv, out_sem,
):
    section = lax.axis_index("section")
    strip = lax.axis_index("strip")
    micro, rows, cols, channels = result.shape
    middle = sections // 2
    is_first = section == 0
    has_next = section + 1 < sections
    has_above = strip > 0
    has_below = strip + 1 < strips
    sends_skip = (section > 0) & (section < middle)
    takes_skip = section > middle
    mirror = sections - section

    weights = (
        pltpu.make_async_copy(conv_first.at[0], first_w, weight_sem.at[0]),
        pltpu.make_async_copy(conv_second.at[0], second_w, weight_sem.at[1]),
        pltpu.make_async_copy(bias_first, first_b, weight_sem.at[2]),
        pltpu.make_async_copy(bias_second, second_b, weight_sem.at[3]),
    )
    skip_weight = pltpu.make_async_copy(conv_skip.at[0], skip_w, weight_sem.at[4])
    own_rows = pltpu.make_async_copy(images, land.at[:, pl.ds(HALO, rows)], image_sem)

    inner_below = lax.rem(strip, 2) == 0
    half = rows // 2
    outer_row = jnp.where(inner_below, 0, rows - half)
    inner_row = jnp.where(inner_below, rows - half, 0)

    def onward(m, part):
        row = (outer_row, inner_row)[part]
        return pltpu.make_async_remote_copy(
            src_ref=result.at[m, pl.ds(row, half)], dst_ref=land.at[m, pl.ds(HALO + row, half)],
            send_sem=land_send.at[m, part], recv_sem=land_recv.at[m, part],
            device_id=(section + 1, strip), device_id_type=MESH)

    def skipped(m):
        return pltpu.make_async_remote_copy(
            src_ref=land.at[m, pl.ds(HALO, rows)], dst_ref=skip_land.at[m, pl.ds(HALO, rows)],
            send_sem=skip_send.at[m], recv_sem=skip_recv.at[m],
            device_id=(mirror, strip), device_id_type=MESH)

    def edge(m, of_skip, direction):
        buffer = skip_land if of_skip else land
        send, recv = (skip_edge_send, skip_edge_recv) if of_skip else (edge_send, edge_recv)
        source, target = ((HALO, HALO + rows), (rows, 0))[direction]
        return pltpu.make_async_remote_copy(
            src_ref=buffer.at[m, pl.ds(source, HALO)], dst_ref=buffer.at[m, pl.ds(target, HALO)],
            send_sem=send.at[m, direction], recv_sem=recv.at[m, direction],
            device_id=(section, strip + 2 * direction - 1), device_id_type=MESH)

    def pass_on(m, of_skip=False, to_above=True, to_below=True):
        @pl.when(has_above & to_above)
        def _():
            edge(m, of_skip, 0).start()

        @pl.when(has_below & to_below)
        def _():
            edge(m, of_skip, 1).start()

    def receive_edges(m, of_skip=False):
        @pl.when(has_below)
        def _():
            edge(m, of_skip, 0).wait_recv()

        @pl.when(has_above)
        def _():
            edge(m, of_skip, 1).wait_recv()

    def sent_edges(m, of_skip=False):
        @pl.when(has_above)
        def _():
            edge(m, of_skip, 0).wait_send()

        @pl.when(has_below)
        def _():
            edge(m, of_skip, 1).wait_send()

    def receive_strip(m):
        @pl.when(section > 0)
        def _():
            onward(m, 0).wait_recv()
            pass_on(m, False, inner_below, jnp.logical_not(inner_below))
            onward(m, 1).wait_recv()
            pass_on(m, False, jnp.logical_not(inner_below), inner_below)

    for copy in weights:
        copy.start()
    pl.when(section >= middle)(skip_weight.start)
    pl.when(is_first)(own_rows.start)

    barrier = pltpu.get_barrier_semaphore()

    def greet(condition, to_section, to_strip):
        @pl.when(condition)
        def _():
            pl.semaphore_signal(barrier, inc=1, device_id=(to_section, to_strip), device_id_type=MESH)

    greet(has_above, section, strip - 1)
    greet(has_below, section, strip + 1)
    greet(section > 0, section - 1, strip)
    greet(takes_skip, mirror, strip)
    expected = sum(
        condition.astype(jnp.int32) for condition in (has_above, has_below, has_next, sends_skip)
    )

    @pl.when(expected > 0)
    def _():
        pl.semaphore_wait(barrier, expected)

    @pl.when(is_first)
    def _():
        own_rows.wait()
        for m in range(micro):
            pass_on(m)

    blank = jnp.zeros((micro, HALO, cols, channels), land.dtype)

    @pl.when(jnp.logical_not(has_above))
    def _():
        land[:, 0:HALO] = blank
        skip_land[:, 0:HALO] = blank

    @pl.when(jnp.logical_not(has_below))
    def _():
        land[:, HALO + rows:] = blank
        skip_land[:, HALO + rows:] = blank

    pl.when(section >= middle)(skip_weight.wait)
    for copy in weights:
        copy.wait()

    @pl.when(section == middle)
    def _():
        def add(tap, carry):
            total = first_w[tap].astype(jnp.float32) + skip_w[tap].astype(jnp.float32)
            first_w[tap] = total.astype(first_w.dtype)
            return carry
        lax.fori_loop(0, 9, add, 0)

    def convolve(window, weight, out_rows):
        size = out_rows * cols
        shape = (out_rows, cols, channels)
        read = jnp.concatenate([window(a).reshape(size, channels) for a in range(3)], axis=1)
        column = lax.broadcasted_iota(jnp.int32, shape, 1)

        def product(b):
            taps = jnp.concatenate([weight[3 * a + b] for a in range(3)], axis=0)
            return jnp.dot(read, taps, preferred_element_type=jnp.float32)

        def moved(value, distance, edge_column):
            rolled = pltpu.roll(value, distance % size, axis=0).reshape(shape)
            return jnp.where(column == edge_column, 0.0, rolled)

        left = moved(product(0), 1, 0)
        right = moved(product(2), -1, cols - 1)
        return left + right + product(1).reshape(shape)

    hidden_rows = rows + 2
    first_bias = first_b[...].reshape(1, 1, channels)
    second_bias = second_b[...].reshape(1, 1, channels)

    @pl.when(takes_skip)
    def _():
        for m in range(micro):
            skipped(m).wait_recv()
            pass_on(m, True)

        def skip_step(m, carry):
            receive_edges(m, True)
            pre[m] = first_bias + convolve(
                lambda a: skip_land[m, pl.ds(a, hidden_rows)], skip_w, hidden_rows)
            return carry

        lax.fori_loop(0, micro, skip_step, 0)

    @pl.when(jnp.logical_not(takes_skip))
    def _():
        pre[...] = jnp.broadcast_to(first_bias, pre.shape)

    receive_strip(0)

    def step(m, carry):
        receive_edges(m)
        hidden = convolve(lambda a: land[m, pl.ds(a, hidden_rows)], first_w, hidden_rows)
        hidden = jnp.maximum(hidden + pre[m], 0.0)
        row = lax.broadcasted_iota(jnp.int32, hidden.shape, 0)
        least = jnp.where(has_above, 0, 1)
        most = jnp.where(has_below, hidden_rows, hidden_rows - 1)
        hidden = jnp.where((row >= least) & (row < most), hidden, 0.0).astype(jnp.bfloat16)
        hidden_map[...] = hidden

        @pl.when(m + 1 < micro)
        def _():
            receive_strip(m + 1)

        final = convolve(lambda a: hidden_map[pl.ds(a, rows)], second_w, rows)
        result[m] = jnp.maximum(final + second_bias, 0.0).astype(jnp.bfloat16)

        @pl.when(has_next)
        def _():
            onward(m, 0).start()
            onward(m, 1).start()

        @pl.when(sends_skip)
        def _():
            skipped(m).start()

        pltpu.make_async_copy(result.at[m], out.at[0, m], out_sem.at[m]).start()
        return carry

    lax.fori_loop(0, micro, step, 0)

    for m in range(micro):
        pltpu.make_async_copy(result.at[m], out.at[0, m], out_sem.at[m]).wait()

        sent_edges(m)

        @pl.when(takes_skip)
        def _():
            sent_edges(m, True)

        @pl.when(has_next)
        def _():
            onward(m, 0).wait_send()
            onward(m, 1).wait_send()

        @pl.when(sends_skip)
        def _():
            skipped(m).wait_send()


def body(images, conv_first, conv_skip, conv_second, bias_first, bias_second):
    sections = lax.axis_size("section")
    strips = lax.axis_size("strip")
    micro, rows, cols, channels = images.shape
    padded = (micro, rows + 2 * HALO, cols, channels)
    weight = conv_first.shape[1:]
    copies = pltpu.SemaphoreType.DMA((micro, 2))
    pixels = rows * cols
    flops = 2 * micro * 2 * pixels * channels * channels * 9
    return pl.pallas_call(
        functools.partial(kernel, sections, strips),
        out_shape=jax.ShapeDtypeStruct((1, micro, rows, cols, channels), jnp.bfloat16),
        in_specs=[pl.BlockSpec(memory_space=pltpu.HBM)] * 6,
        out_specs=pl.BlockSpec(memory_space=pltpu.HBM),
        scratch_shapes=[
            pltpu.VMEM(weight, jnp.bfloat16),
            pltpu.VMEM(weight, jnp.bfloat16),
            pltpu.VMEM(weight, jnp.bfloat16),
            pltpu.VMEM((1, channels), jnp.float32),
            pltpu.VMEM((1, channels), jnp.float32),
            pltpu.VMEM(padded, jnp.bfloat16),
            pltpu.VMEM(padded, jnp.bfloat16),
            pltpu.VMEM((micro, rows, cols, channels), jnp.bfloat16),
            pltpu.VMEM((rows + 2, cols, channels), jnp.bfloat16),
            pltpu.VMEM((micro, rows + 2, cols, channels), jnp.float32),
            pltpu.SemaphoreType.DMA((5,)),
            pltpu.SemaphoreType.DMA,
            copies, copies, copies, copies, copies, copies,
            pltpu.SemaphoreType.DMA((micro,)),
            pltpu.SemaphoreType.DMA((micro,)),
            pltpu.SemaphoreType.DMA((micro,)),
        ],
        compiler_params=pltpu.CompilerParams(
            collective_id=0, has_side_effects=True
        ),
        cost_estimate=pl.CostEstimate(
            flops=flops, bytes_accessed=3 * conv_first.size * 2, transcendentals=0
        ),
    )(images, conv_first, conv_skip, conv_second, bias_first, bias_second)


def solution(mesh):
    placed = (
        P(None, "strip", None, None),
        P("section", None, None, None),
        P("section", None, None, None),
        P("section", None, None, None),
        P("section", None),
        P("section", None),
    )
    return jax.shard_map(
        body,
        mesh=mesh,
        in_specs=placed,
        out_specs=P("section", None, "strip", None, None),
        check_vma=False,
    )
```

```python
import functools

import jax
import jax.numpy as jnp
from jax import lax
from jax.experimental import pallas as pl
from jax.experimental.pallas import tpu as pltpu
from jax.sharding import PartitionSpec as P

MESH = pl.DeviceIdType.MESH
HALO = 2


def kernel(
    sections, strips,
    images, conv_first, conv_skip, conv_second, bias_first, bias_second,
    out,
    first_w, skip_w, second_w, first_b, second_b,
    land, skip_land, result, hidden_map, pre,
    weight_sem, image_sem, first_send, edge_send, edge_recv, land_send, land_recv, skip_send, skip_recv, out_sem,
):
    section = lax.axis_index("section")
    strip = lax.axis_index("strip")
    micro, rows, cols, channels = result.shape
    middle = sections // 2
    is_first = section == 0
    has_next = section + 1 < sections
    has_above = strip > 0
    has_below = strip + 1 < strips
    sends_skip = (section > 0) & (section < middle)
    takes_skip = section > middle
    mirror = sections - section

    weights = (
        pltpu.make_async_copy(conv_first.at[0], first_w, weight_sem.at[0]),
        pltpu.make_async_copy(conv_second.at[0], second_w, weight_sem.at[1]),
        pltpu.make_async_copy(bias_first, first_b, weight_sem.at[2]),
        pltpu.make_async_copy(bias_second, second_b, weight_sem.at[3]),
    )
    skip_weight = pltpu.make_async_copy(conv_skip.at[0], skip_w, weight_sem.at[4])
    own_rows = pltpu.make_async_copy(images, land.at[:, pl.ds(HALO, rows)], image_sem)

    even = lax.rem(strip, 2) == 0
    inner = jnp.where(even, strip + 1, strip - 1)
    outer = jnp.where(even, strip - 1, strip + 1)
    has_inner = inner < strips
    has_outer = jnp.where(even, has_above, has_below)
    half = rows // 2
    inner_row = jnp.where(even, rows - half, 0)
    outer_row = jnp.where(even, 0, rows - half)
    inner_edge = jnp.where(even, rows - HALO, 0)
    outer_edge = jnp.where(even, 0, rows - HALO)
    inner_halo = jnp.where(even, 0, HALO + rows)
    outer_halo = jnp.where(even, HALO + rows, 0)

    def halves(m):
        return [pltpu.make_async_remote_copy(
            src_ref=result.at[m, pl.ds(row, half)], dst_ref=land.at[m, pl.ds(HALO + row, half)],
            send_sem=land_send.at[m, part], recv_sem=land_recv.at[m, part],
            device_id=(section + 1, strip), device_id_type=MESH)
            for part, row in enumerate((inner_row, outer_row))]

    def edge(m, source, to_section, part):
        send = first_send if source is images else edge_send
        row, halo, to_strip = ((inner_edge, inner_halo, inner), (outer_edge, outer_halo, outer))[part]
        return pltpu.make_async_remote_copy(
            src_ref=source.at[m, pl.ds(row, HALO)], dst_ref=land.at[m, pl.ds(halo, HALO)],
            send_sem=send.at[m, part], recv_sem=edge_recv.at[m, part],
            device_id=(to_section, to_strip), device_id_type=MESH)

    def send_edges(m, source, to_section):
        @pl.when(has_outer)
        def _():
            edge(m, source, to_section, 1).start()

        @pl.when(has_inner)
        def _():
            edge(m, source, to_section, 0).start()

    def receive_edges(m):
        @pl.when(has_outer)
        def _():
            edge(m, result, section, 1).wait_recv()

        @pl.when(has_inner)
        def _():
            edge(m, result, section, 0).wait_recv()

    def sent_edges(m, source):
        @pl.when(has_outer)
        def _():
            edge(m, source, section, 1).wait_send()

        @pl.when(has_inner)
        def _():
            edge(m, source, section, 0).wait_send()

    def skipped(m):
        return pltpu.make_async_remote_copy(
            src_ref=land.at[m], dst_ref=skip_land.at[m],
            send_sem=skip_send.at[m], recv_sem=skip_recv.at[m],
            device_id=(mirror, strip), device_id_type=MESH)

    for copy in weights:
        copy.start()
    pl.when(section >= middle)(skip_weight.start)
    pl.when(is_first)(own_rows.start)

    barrier = pltpu.get_barrier_semaphore()

    def greet(condition, to_section, to_strip):
        @pl.when(condition)
        def _():
            pl.semaphore_signal(barrier, inc=1, device_id=(to_section, to_strip), device_id_type=MESH)

    for condition, to_strip in ((has_inner, inner), (has_outer, outer)):
        greet(is_first & condition, section, to_strip)
        greet((section > 0) & condition, section - 1, to_strip)
    greet(section > 0, section - 1, strip)
    greet(takes_skip, mirror, strip)
    beside = has_inner.astype(jnp.int32) + has_outer.astype(jnp.int32)
    expected = (
        jnp.where(is_first, beside, 0)
        + jnp.where(has_next, beside + 1, 0)
        + jnp.where(sends_skip, 1, 0)
    )

    @pl.when(expected > 0)
    def _():
        pl.semaphore_wait(barrier, expected)

    @pl.when(is_first)
    def _():
        for m in range(micro):
            send_edges(m, images, section)

    blank = jnp.zeros((micro, HALO, cols, channels), land.dtype)

    @pl.when(jnp.logical_not(has_above))
    def _():
        land[:, 0:HALO] = blank

    @pl.when(jnp.logical_not(has_below))
    def _():
        land[:, HALO + rows:] = blank

    pl.when(section >= middle)(skip_weight.wait)
    for copy in weights:
        copy.wait()

    @pl.when(section == middle)
    def _():
        def add(tap, carry):
            total = first_w[tap].astype(jnp.float32) + skip_w[tap].astype(jnp.float32)
            first_w[tap] = total.astype(first_w.dtype)
            return carry
        lax.fori_loop(0, 9, add, 0)

    def convolve(window, weight, out_rows):
        size = out_rows * cols
        shape = (out_rows, cols, channels)
        read = jnp.concatenate([window(a).reshape(size, channels) for a in range(3)], axis=1)
        column = lax.broadcasted_iota(jnp.int32, shape, 1)

        def product(b):
            taps = jnp.concatenate([weight[3 * a + b] for a in range(3)], axis=0)
            return jnp.dot(read, taps, preferred_element_type=jnp.float32)

        def moved(value, distance, edge_column):
            rolled = pltpu.roll(value, distance % size, axis=0).reshape(shape)
            return jnp.where(column == edge_column, 0.0, rolled)

        left = moved(product(0), 1, 0)
        right = moved(product(2), -1, cols - 1)
        return left + right + product(1).reshape(shape)

    hidden_rows = rows + 2
    first_bias = first_b[...].reshape(1, 1, channels)
    second_bias = second_b[...].reshape(1, 1, channels)

    @pl.when(takes_skip)
    def _():
        for m in range(micro):
            skipped(m).wait_recv()

        def skip_step(m, carry):
            pre[m] = first_bias + convolve(
                lambda a: skip_land[m, pl.ds(a, hidden_rows)], skip_w, hidden_rows)
            return carry

        lax.fori_loop(0, micro, skip_step, 0)

    @pl.when(jnp.logical_not(takes_skip))
    def _():
        pre[...] = jnp.broadcast_to(first_bias, pre.shape)

    pl.when(is_first)(own_rows.wait)

    def step(m, carry):
        @pl.when(section > 0)
        def _():
            for copy in halves(m):
                copy.wait_recv()

        receive_edges(m)
        hidden = convolve(lambda a: land[m, pl.ds(a, hidden_rows)], first_w, hidden_rows)
        hidden = jnp.maximum(hidden + pre[m], 0.0)
        row = lax.broadcasted_iota(jnp.int32, hidden.shape, 0)
        least = jnp.where(has_above, 0, 1)
        most = jnp.where(has_below, hidden_rows, hidden_rows - 1)
        hidden = jnp.where((row >= least) & (row < most), hidden, 0.0).astype(jnp.bfloat16)
        hidden_map[...] = hidden

        final = convolve(lambda a: hidden_map[pl.ds(a, rows)], second_w, rows)
        result[m] = jnp.maximum(final + second_bias, 0.0).astype(jnp.bfloat16)

        @pl.when(has_next)
        def _():
            send_edges(m, result, section + 1)
            for copy in halves(m):
                copy.start()

        @pl.when(sends_skip)
        def _():
            skipped(m).start()

        pltpu.make_async_copy(result.at[m], out.at[0, m], out_sem.at[m]).start()
        return carry

    lax.fori_loop(0, micro, step, 0)

    for m in range(micro):
        pltpu.make_async_copy(result.at[m], out.at[0, m], out_sem.at[m]).wait()

        @pl.when(is_first)
        def _():
            sent_edges(m, images)

        @pl.when(has_next)
        def _():
            for copy in halves(m):
                copy.wait_send()
            sent_edges(m, result)

        @pl.when(sends_skip)
        def _():
            skipped(m).wait_send()


def body(images, conv_first, conv_skip, conv_second, bias_first, bias_second):
    sections = lax.axis_size("section")
    strips = lax.axis_size("strip")
    micro, rows, cols, channels = images.shape
    padded = (micro, rows + 2 * HALO, cols, channels)
    weight = conv_first.shape[1:]
    copies = pltpu.SemaphoreType.DMA((micro, 2))
    pixels = rows * cols
    flops = 2 * micro * 2 * pixels * channels * channels * 9
    return pl.pallas_call(
        functools.partial(kernel, sections, strips),
        out_shape=jax.ShapeDtypeStruct((1, micro, rows, cols, channels), jnp.bfloat16),
        in_specs=[pl.BlockSpec(memory_space=pltpu.HBM)] * 6,
        out_specs=pl.BlockSpec(memory_space=pltpu.HBM),
        scratch_shapes=[
            pltpu.VMEM(weight, jnp.bfloat16),
            pltpu.VMEM(weight, jnp.bfloat16),
            pltpu.VMEM(weight, jnp.bfloat16),
            pltpu.VMEM((1, channels), jnp.float32),
            pltpu.VMEM((1, channels), jnp.float32),
            pltpu.VMEM(padded, jnp.bfloat16),
            pltpu.VMEM(padded, jnp.bfloat16),
            pltpu.VMEM((micro, rows, cols, channels), jnp.bfloat16),
            pltpu.VMEM((rows + 2, cols, channels), jnp.bfloat16),
            pltpu.VMEM((micro, rows + 2, cols, channels), jnp.float32),
            pltpu.SemaphoreType.DMA((5,)),
            pltpu.SemaphoreType.DMA,
            copies, copies, copies, copies, copies,
            pltpu.SemaphoreType.DMA((micro,)),
            pltpu.SemaphoreType.DMA((micro,)),
            pltpu.SemaphoreType.DMA((micro,)),
        ],
        compiler_params=pltpu.CompilerParams(
            collective_id=0, has_side_effects=True
        ),
        cost_estimate=pl.CostEstimate(
            flops=flops, bytes_accessed=3 * conv_first.size * 2, transcendentals=0
        ),
    )(images, conv_first, conv_skip, conv_second, bias_first, bias_second)


def solution(mesh):
    placed = (
        P(None, "strip", None, None),
        P("section", None, None, None),
        P("section", None, None, None),
        P("section", None, None, None),
        P("section", None),
        P("section", None),
    )
    return jax.shard_map(
        body,
        mesh=mesh,
        in_specs=placed,
        out_specs=P("section", None, "strip", None, None),
        check_vma=False,
    )
```

```python
import functools

import jax
import jax.numpy as jnp
from jax import lax
from jax.experimental import pallas as pl
from jax.experimental.pallas import tpu as pltpu
from jax.sharding import PartitionSpec as P

MESH = pl.DeviceIdType.MESH
HALO = 2


def kernel(
    sections, strips,
    images, conv_first, conv_skip, conv_second, bias_first, bias_second,
    out,
    first_w, skip_w, second_w, first_b, second_b,
    land, skip_land, result, hidden_map, pre,
    weight_sem, image_sem, own_send, edge_send, edge_recv, land_send, land_recv, skip_send, skip_recv, out_sem,
):
    section = lax.axis_index("section")
    strip = lax.axis_index("strip")
    micro, rows, cols, channels = result.shape
    middle = sections // 2
    is_first = section == 0
    has_next = section + 1 < sections
    has_above = strip > 0
    has_below = strip + 1 < strips
    sends_skip = (section > 0) & (section < middle)
    takes_skip = section > middle
    mirror = sections - section

    weights = (
        pltpu.make_async_copy(conv_first.at[0], first_w, weight_sem.at[0]),
        pltpu.make_async_copy(conv_second.at[0], second_w, weight_sem.at[1]),
        pltpu.make_async_copy(bias_first, first_b, weight_sem.at[2]),
        pltpu.make_async_copy(bias_second, second_b, weight_sem.at[3]),
    )
    skip_weight = pltpu.make_async_copy(conv_skip.at[0], skip_w, weight_sem.at[4])
    own_rows = pltpu.make_async_copy(images, land.at[:, pl.ds(HALO, rows)], image_sem)

    even = lax.rem(strip, 2) == 0
    inner = jnp.where(even, strip + 1, strip - 1)
    outer = jnp.where(even, strip - 1, strip + 1)
    has_inner = inner < strips
    has_outer = jnp.where(even, has_above, has_below)
    half = rows // 2
    inner_row = jnp.where(even, rows - half, 0)
    outer_row = jnp.where(even, 0, rows - half)
    inner_edge = jnp.where(even, rows - HALO, 0)
    outer_edge = jnp.where(even, 0, rows - HALO)
    inner_halo = jnp.where(even, 0, HALO + rows)
    outer_halo = jnp.where(even, HALO + rows, 0)

    def halves(m):
        return [pltpu.make_async_remote_copy(
            src_ref=result.at[m, pl.ds(row, half)], dst_ref=land.at[m, pl.ds(HALO + row, half)],
            send_sem=land_send.at[m, part], recv_sem=land_recv.at[m, part],
            device_id=(section + 1, strip), device_id_type=MESH)
            for part, row in enumerate((inner_row, outer_row))]

    def edge(m, source, to_section, part):
        send = edge_send if source is result else own_send
        row, halo, to_strip = ((inner_edge, inner_halo, inner), (outer_edge, outer_halo, outer))[part]
        return pltpu.make_async_remote_copy(
            src_ref=source.at[m, pl.ds(row, HALO)], dst_ref=land.at[m, pl.ds(halo, HALO)],
            send_sem=send.at[m, part], recv_sem=edge_recv.at[m, part],
            device_id=(to_section, to_strip), device_id_type=MESH)

    def start_outer(m, source, to_section):
        @pl.when(has_outer)
        def _():
            edge(m, source, to_section, 1).start()

    def start_inner(m, source):
        @pl.when(has_inner)
        def _():
            edge(m, source, section, 0).start()

    def receive_edges(m):
        @pl.when(has_outer)
        def _():
            edge(m, result, section, 1).wait_recv()

        @pl.when(has_inner)
        def _():
            edge(m, result, section, 0).wait_recv()

    def sent_outer(m, source):
        @pl.when(has_outer)
        def _():
            edge(m, source, section, 1).wait_send()

    def sent_inner(m):
        @pl.when(has_inner)
        def _():
            edge(m, images, section, 0).wait_send()

    landed = land.at[:, pl.ds(HALO, rows)]

    def skipped(m):
        return pltpu.make_async_remote_copy(
            src_ref=land.at[m], dst_ref=skip_land.at[m],
            send_sem=skip_send.at[m], recv_sem=skip_recv.at[m],
            device_id=(mirror, strip), device_id_type=MESH)

    for copy in weights:
        copy.start()
    pl.when(section >= middle)(skip_weight.start)
    pl.when(is_first)(own_rows.start)

    barrier = pltpu.get_barrier_semaphore()

    def greet(condition, to_section, to_strip):
        @pl.when(condition)
        def _():
            pl.semaphore_signal(barrier, inc=1, device_id=(to_section, to_strip), device_id_type=MESH)

    greet(has_inner, section, inner)
    greet(has_outer, jnp.where(is_first, section, section - 1), outer)
    greet(section > 0, section - 1, strip)
    greet(takes_skip, mirror, strip)
    inner_count, outer_count = has_inner.astype(jnp.int32), has_outer.astype(jnp.int32)
    expected = (
        inner_count
        + jnp.where(is_first, outer_count, 0)
        + jnp.where(has_next, outer_count + 1, 0)
        + jnp.where(sends_skip, 1, 0)
    )

    @pl.when(expected > 0)
    def _():
        pl.semaphore_wait(barrier, expected)

    @pl.when(is_first)
    def _():
        for m in range(micro):
            start_outer(m, images, section)
            start_inner(m, images)

    blank = jnp.zeros((micro, HALO, cols, channels), land.dtype)

    @pl.when(jnp.logical_not(has_above))
    def _():
        land[:, 0:HALO] = blank

    @pl.when(jnp.logical_not(has_below))
    def _():
        land[:, HALO + rows:] = blank

    pl.when(section >= middle)(skip_weight.wait)
    for copy in weights:
        copy.wait()

    @pl.when(section == middle)
    def _():
        def add(tap, carry):
            total = first_w[tap].astype(jnp.float32) + skip_w[tap].astype(jnp.float32)
            first_w[tap] = total.astype(first_w.dtype)
            return carry
        lax.fori_loop(0, 9, add, 0)

    def convolve(window, weight, out_rows):
        size = out_rows * cols
        shape = (out_rows, cols, channels)
        read = jnp.concatenate([window(a).reshape(size, channels) for a in range(3)], axis=1)
        column = lax.broadcasted_iota(jnp.int32, shape, 1)

        def product(b):
            taps = jnp.concatenate([weight[3 * a + b] for a in range(3)], axis=0)
            return jnp.dot(read, taps, preferred_element_type=jnp.float32)

        def moved(value, distance, edge_column):
            rolled = pltpu.roll(value, distance % size, axis=0).reshape(shape)
            return jnp.where(column == edge_column, 0.0, rolled)

        left = moved(product(0), 1, 0)
        right = moved(product(2), -1, cols - 1)
        return left + right + product(1).reshape(shape)

    hidden_rows = rows + 2
    first_bias = first_b[...].reshape(1, 1, channels)
    second_bias = second_b[...].reshape(1, 1, channels)

    @pl.when(takes_skip)
    def _():
        for m in range(micro):
            skipped(m).wait_recv()

        def skip_step(m, carry):
            pre[m] = first_bias + convolve(
                lambda a: skip_land[m, pl.ds(a, hidden_rows)], skip_w, hidden_rows)
            return carry

        lax.fori_loop(0, micro, skip_step, 0)

    @pl.when(jnp.logical_not(takes_skip))
    def _():
        pre[...] = jnp.broadcast_to(first_bias, pre.shape)

    pl.when(is_first)(own_rows.wait)

    def step(m, carry):
        @pl.when(section > 0)
        def _():
            inner_half, outer_half = halves(m)
            inner_half.wait_recv()
            start_inner(m, landed)
            outer_half.wait_recv()

        receive_edges(m)
        hidden = convolve(lambda a: land[m, pl.ds(a, hidden_rows)], first_w, hidden_rows)
        hidden = jnp.maximum(hidden + pre[m], 0.0)
        row = lax.broadcasted_iota(jnp.int32, hidden.shape, 0)
        least = jnp.where(has_above, 0, 1)
        most = jnp.where(has_below, hidden_rows, hidden_rows - 1)
        hidden = jnp.where((row >= least) & (row < most), hidden, 0.0).astype(jnp.bfloat16)
        hidden_map[...] = hidden

        final = convolve(lambda a: hidden_map[pl.ds(a, rows)], second_w, rows)
        result[m] = jnp.maximum(final + second_bias, 0.0).astype(jnp.bfloat16)

        @pl.when(has_next)
        def _():
            start_outer(m, result, section + 1)
            for copy in halves(m):
                copy.start()

        @pl.when(sends_skip)
        def _():
            skipped(m).start()

        pltpu.make_async_copy(result.at[m], out.at[0, m], out_sem.at[m]).start()
        return carry

    lax.fori_loop(0, micro, step, 0)

    for m in range(micro):
        pltpu.make_async_copy(result.at[m], out.at[0, m], out_sem.at[m]).wait()

        sent_inner(m)

        @pl.when(is_first)
        def _():
            sent_outer(m, images)

        @pl.when(has_next)
        def _():
            for copy in halves(m):
                copy.wait_send()
            sent_outer(m, result)

        @pl.when(sends_skip)
        def _():
            skipped(m).wait_send()


def body(images, conv_first, conv_skip, conv_second, bias_first, bias_second):
    sections = lax.axis_size("section")
    strips = lax.axis_size("strip")
    micro, rows, cols, channels = images.shape
    padded = (micro, rows + 2 * HALO, cols, channels)
    weight = conv_first.shape[1:]
    copies = pltpu.SemaphoreType.DMA((micro, 2))
    pixels = rows * cols
    flops = 2 * micro * 2 * pixels * channels * channels * 9
    return pl.pallas_call(
        functools.partial(kernel, sections, strips),
        out_shape=jax.ShapeDtypeStruct((1, micro, rows, cols, channels), jnp.bfloat16),
        in_specs=[pl.BlockSpec(memory_space=pltpu.HBM)] * 6,
        out_specs=pl.BlockSpec(memory_space=pltpu.HBM),
        scratch_shapes=[
            pltpu.VMEM(weight, jnp.bfloat16),
            pltpu.VMEM(weight, jnp.bfloat16),
            pltpu.VMEM(weight, jnp.bfloat16),
            pltpu.VMEM((1, channels), jnp.float32),
            pltpu.VMEM((1, channels), jnp.float32),
            pltpu.VMEM(padded, jnp.bfloat16),
            pltpu.VMEM(padded, jnp.bfloat16),
            pltpu.VMEM((micro, rows, cols, channels), jnp.bfloat16),
            pltpu.VMEM((rows + 2, cols, channels), jnp.bfloat16),
            pltpu.VMEM((micro, rows + 2, cols, channels), jnp.float32),
            pltpu.SemaphoreType.DMA((5,)),
            pltpu.SemaphoreType.DMA,
            copies, copies, copies, copies, copies,
            pltpu.SemaphoreType.DMA((micro,)),
            pltpu.SemaphoreType.DMA((micro,)),
            pltpu.SemaphoreType.DMA((micro,)),
        ],
        compiler_params=pltpu.CompilerParams(
            collective_id=0, has_side_effects=True
        ),
        cost_estimate=pl.CostEstimate(
            flops=flops, bytes_accessed=3 * conv_first.size * 2, transcendentals=0
        ),
    )(images, conv_first, conv_skip, conv_second, bias_first, bias_second)


def solution(mesh):
    placed = (
        P(None, "strip", None, None),
        P("section", None, None, None),
        P("section", None, None, None),
        P("section", None, None, None),
        P("section", None),
        P("section", None),
    )
    return jax.shard_map(
        body,
        mesh=mesh,
        in_specs=placed,
        out_specs=P("section", None, "strip", None, None),
        check_vma=False,
    )
```

```python
import functools

import jax
import jax.numpy as jnp
from jax import lax
from jax.experimental import pallas as pl
from jax.experimental.pallas import tpu as pltpu
from jax.sharding import PartitionSpec as P

MESH = pl.DeviceIdType.MESH
HALO = 2


def kernel(
    sections, strips,
    images, conv_first, conv_skip, conv_second, bias_first, bias_second,
    out,
    first_w, skip_w, second_w, first_b, second_b,
    land, skip_land, result, hidden_map, pre,
    weight_sem, image_sem, own_send, edge_send, edge_recv, skip_edge_send, skip_edge_recv, land_send, land_recv, skip_send, skip_recv, out_sem,
):
    section = lax.axis_index("section")
    strip = lax.axis_index("strip")
    micro, rows, cols, channels = result.shape
    middle = sections // 2
    is_first = section == 0
    has_next = section + 1 < sections
    has_above = strip > 0
    has_below = strip + 1 < strips
    sends_skip = (section > 0) & (section < middle)
    takes_skip = section > middle
    mirror = sections - section

    weights = (
        pltpu.make_async_copy(conv_first.at[0], first_w, weight_sem.at[0]),
        pltpu.make_async_copy(conv_second.at[0], second_w, weight_sem.at[1]),
        pltpu.make_async_copy(bias_first, first_b, weight_sem.at[2]),
        pltpu.make_async_copy(bias_second, second_b, weight_sem.at[3]),
    )
    skip_weight = pltpu.make_async_copy(conv_skip.at[0], skip_w, weight_sem.at[4])
    own_rows = pltpu.make_async_copy(images, land.at[:, pl.ds(HALO, rows)], image_sem)

    even = lax.rem(strip, 2) == 0
    inner = jnp.where(even, strip + 1, strip - 1)
    outer = jnp.where(even, strip - 1, strip + 1)
    has_inner = inner < strips
    has_outer = jnp.where(even, has_above, has_below)
    half = rows // 2
    inner_row = jnp.where(even, rows - half, 0)
    outer_row = jnp.where(even, 0, rows - half)
    inner_edge = jnp.where(even, rows - HALO, 0)
    outer_edge = jnp.where(even, 0, rows - HALO)
    inner_halo = jnp.where(even, 0, HALO + rows)
    outer_halo = jnp.where(even, HALO + rows, 0)

    def halves(m):
        return [pltpu.make_async_remote_copy(
            src_ref=result.at[m, pl.ds(row, half)], dst_ref=land.at[m, pl.ds(HALO + row, half)],
            send_sem=land_send.at[m, part], recv_sem=land_recv.at[m, part],
            device_id=(section + 1, strip), device_id_type=MESH)
            for part, row in enumerate((inner_row, outer_row))]

    def edge(m, source, to_section, part):
        send = edge_send if source is result else own_send
        row, halo, to_strip = ((inner_edge, inner_halo, inner), (outer_edge, outer_halo, outer))[part]
        return pltpu.make_async_remote_copy(
            src_ref=source.at[m, pl.ds(row, HALO)], dst_ref=land.at[m, pl.ds(halo, HALO)],
            send_sem=send.at[m, part], recv_sem=edge_recv.at[m, part],
            device_id=(to_section, to_strip), device_id_type=MESH)

    def start_outer(m, source, to_section):
        @pl.when(has_outer)
        def _():
            edge(m, source, to_section, 1).start()

    def start_inner(m, source):
        @pl.when(has_inner)
        def _():
            edge(m, source, section, 0).start()

    def receive_edges(m):
        @pl.when(has_outer)
        def _():
            edge(m, result, section, 1).wait_recv()

        @pl.when(has_inner)
        def _():
            edge(m, result, section, 0).wait_recv()

    def sent_outer(m, source):
        @pl.when(has_outer)
        def _():
            edge(m, source, section, 1).wait_send()

    def sent_inner(m):
        @pl.when(has_inner)
        def _():
            edge(m, images, section, 0).wait_send()

    def skip_edge(m, part):
        row, halo, to_strip = ((inner_edge, inner_halo, inner), (outer_edge, outer_halo, outer))[part]
        return pltpu.make_async_remote_copy(
            src_ref=skip_land.at[m, pl.ds(HALO + row, HALO)], dst_ref=skip_land.at[m, pl.ds(halo, HALO)],
            send_sem=skip_edge_send.at[m, part], recv_sem=skip_edge_recv.at[m, part],
            device_id=(section, to_strip), device_id_type=MESH)

    beside = ((has_inner, 0), (has_outer, 1))

    landed = land.at[:, pl.ds(HALO, rows)]

    def skipped(m):
        return pltpu.make_async_remote_copy(
            src_ref=land.at[m, pl.ds(HALO, rows)], dst_ref=skip_land.at[m, pl.ds(HALO, rows)],
            send_sem=skip_send.at[m], recv_sem=skip_recv.at[m],
            device_id=(mirror, strip), device_id_type=MESH)

    for copy in weights:
        copy.start()
    pl.when(section >= middle)(skip_weight.start)
    pl.when(is_first)(own_rows.start)

    barrier = pltpu.get_barrier_semaphore()

    def greet(condition, to_section, to_strip):
        @pl.when(condition)
        def _():
            pl.semaphore_signal(barrier, inc=1, device_id=(to_section, to_strip), device_id_type=MESH)

    greet(has_inner, section, inner)
    greet(has_outer, jnp.where(is_first, section, section - 1), outer)
    greet(section > 0, section - 1, strip)
    greet(takes_skip, mirror, strip)
    greet(takes_skip & has_outer, section, outer)
    inner_count, outer_count = has_inner.astype(jnp.int32), has_outer.astype(jnp.int32)
    expected = (
        inner_count
        + jnp.where(is_first | takes_skip, outer_count, 0)
        + jnp.where(has_next, outer_count + 1, 0)
        + jnp.where(sends_skip, 1, 0)
    )

    @pl.when(expected > 0)
    def _():
        pl.semaphore_wait(barrier, expected)

    @pl.when(is_first)
    def _():
        for m in range(micro):
            start_outer(m, images, section)
            start_inner(m, images)

    blank = jnp.zeros((micro, HALO, cols, channels), land.dtype)

    @pl.when(jnp.logical_not(has_above))
    def _():
        land[:, 0:HALO] = blank
        skip_land[:, 0:HALO] = blank

    @pl.when(jnp.logical_not(has_below))
    def _():
        land[:, HALO + rows:] = blank
        skip_land[:, HALO + rows:] = blank

    pl.when(section >= middle)(skip_weight.wait)
    for copy in weights:
        copy.wait()

    @pl.when(section == middle)
    def _():
        def add(tap, carry):
            total = first_w[tap].astype(jnp.float32) + skip_w[tap].astype(jnp.float32)
            first_w[tap] = total.astype(first_w.dtype)
            return carry
        lax.fori_loop(0, 9, add, 0)

    def convolve(window, weight, out_rows):
        size = out_rows * cols
        shape = (out_rows, cols, channels)
        read = jnp.concatenate([window(a).reshape(size, channels) for a in range(3)], axis=1)
        column = lax.broadcasted_iota(jnp.int32, shape, 1)

        def product(b):
            taps = jnp.concatenate([weight[3 * a + b] for a in range(3)], axis=0)
            return jnp.dot(read, taps, preferred_element_type=jnp.float32)

        def moved(value, distance, edge_column):
            rolled = pltpu.roll(value, distance % size, axis=0).reshape(shape)
            return jnp.where(column == edge_column, 0.0, rolled)

        left = moved(product(0), 1, 0)
        right = moved(product(2), -1, cols - 1)
        return left + right + product(1).reshape(shape)

    hidden_rows = rows + 2
    first_bias = first_b[...].reshape(1, 1, channels)
    second_bias = second_b[...].reshape(1, 1, channels)

    @pl.when(takes_skip)
    def _():
        for m in range(micro):
            skipped(m).wait_recv()
            for condition, part in beside:
                pl.when(condition)(skip_edge(m, part).start)

        def skip_step(m, carry):
            for condition, part in beside:
                pl.when(condition)(skip_edge(m, part).wait_recv)
            pre[m] = first_bias + convolve(
                lambda a: skip_land[m, pl.ds(a, hidden_rows)], skip_w, hidden_rows)
            return carry

        lax.fori_loop(0, micro, skip_step, 0)

    @pl.when(jnp.logical_not(takes_skip))
    def _():
        pre[...] = jnp.broadcast_to(first_bias, pre.shape)

    pl.when(is_first)(own_rows.wait)

    def step(m, carry):
        @pl.when(section > 0)
        def _():
            inner_half, outer_half = halves(m)
            inner_half.wait_recv()
            start_inner(m, landed)
            outer_half.wait_recv()

        @pl.when(sends_skip)
        def _():
            skipped(m).start()

        receive_edges(m)
        hidden = convolve(lambda a: land[m, pl.ds(a, hidden_rows)], first_w, hidden_rows)
        hidden = jnp.maximum(hidden + pre[m], 0.0)
        row = lax.broadcasted_iota(jnp.int32, hidden.shape, 0)
        least = jnp.where(has_above, 0, 1)
        most = jnp.where(has_below, hidden_rows, hidden_rows - 1)
        hidden = jnp.where((row >= least) & (row < most), hidden, 0.0).astype(jnp.bfloat16)
        hidden_map[...] = hidden

        final = convolve(lambda a: hidden_map[pl.ds(a, rows)], second_w, rows)
        result[m] = jnp.maximum(final + second_bias, 0.0).astype(jnp.bfloat16)

        @pl.when(has_next)
        def _():
            start_outer(m, result, section + 1)
            for copy in halves(m):
                copy.start()

        pltpu.make_async_copy(result.at[m], out.at[0, m], out_sem.at[m]).start()
        return carry

    lax.fori_loop(0, micro, step, 0)

    for m in range(micro):
        pltpu.make_async_copy(result.at[m], out.at[0, m], out_sem.at[m]).wait()

        sent_inner(m)

        @pl.when(takes_skip)
        def _():
            for condition, part in beside:
                pl.when(condition)(skip_edge(m, part).wait_send)

        @pl.when(is_first)
        def _():
            sent_outer(m, images)

        @pl.when(has_next)
        def _():
            for copy in halves(m):
                copy.wait_send()
            sent_outer(m, result)

        @pl.when(sends_skip)
        def _():
            skipped(m).wait_send()


def body(images, conv_first, conv_skip, conv_second, bias_first, bias_second):
    sections = lax.axis_size("section")
    strips = lax.axis_size("strip")
    arguments = (images, conv_first, conv_skip, conv_second, bias_first, bias_second)
    micro, rows, cols, channels = images.shape
    padded = (micro, rows + 2 * HALO, cols, channels)
    weight = conv_first.shape[1:]
    copies = pltpu.SemaphoreType.DMA((micro, 2))
    pixels = rows * cols
    flops = 2 * micro * 2 * pixels * channels * channels * 9
    return pl.pallas_call(
        functools.partial(kernel, sections, strips),
        out_shape=jax.ShapeDtypeStruct((1, micro, rows, cols, channels), jnp.bfloat16),
        in_specs=[pl.BlockSpec(memory_space=pltpu.HBM)] * 6,
        out_specs=pl.BlockSpec(memory_space=pltpu.HBM),
        scratch_shapes=[
            pltpu.VMEM(weight, jnp.bfloat16),
            pltpu.VMEM(weight, jnp.bfloat16),
            pltpu.VMEM(weight, jnp.bfloat16),
            pltpu.VMEM((1, channels), jnp.float32),
            pltpu.VMEM((1, channels), jnp.float32),
            pltpu.VMEM(padded, jnp.bfloat16),
            pltpu.VMEM(padded, jnp.bfloat16),
            pltpu.VMEM((micro, rows, cols, channels), jnp.bfloat16),
            pltpu.VMEM((rows + 2, cols, channels), jnp.bfloat16),
            pltpu.VMEM((micro, rows + 2, cols, channels), jnp.float32),
            pltpu.SemaphoreType.DMA((5,)),
            pltpu.SemaphoreType.DMA,
            copies, copies, copies, copies, copies, copies, copies,
            pltpu.SemaphoreType.DMA((micro,)),
            pltpu.SemaphoreType.DMA((micro,)),
            pltpu.SemaphoreType.DMA((micro,)),
        ],
        compiler_params=pltpu.CompilerParams(
            collective_id=0, has_side_effects=True, vmem_limit_bytes=32 * 1024 * 1024
        ),
        cost_estimate=pl.CostEstimate(
            flops=flops, bytes_accessed=3 * conv_first.size * 2, transcendentals=0
        ),
    )(*[pltpu.with_memory_space_constraint(value, pltpu.HBM) for value in arguments])


def solution(mesh):
    placed = (
        P(None, "strip", None, None),
        P("section", None, None, None),
        P("section", None, None, None),
        P("section", None, None, None),
        P("section", None),
        P("section", None),
    )
    return jax.shard_map(
        body,
        mesh=mesh,
        in_specs=placed,
        out_specs=P("section", None, "strip", None, None),
        check_vma=False,
    )
```

```python
import functools

import jax
import jax.numpy as jnp
from jax import lax
from jax.experimental import pallas as pl
from jax.experimental.pallas import tpu as pltpu
from jax.sharding import PartitionSpec as P

MESH = pl.DeviceIdType.MESH
HALO = 2


def kernel(
    sections, strips,
    images, conv_first, conv_skip, conv_second, bias_first, bias_second,
    out,
    first_w, skip_w, second_w, first_b, second_b,
    land, skip_land, result, hidden_map, pre,
    weight_sem, image_sem, own_send, edge_send, edge_recv, skip_edge_send, skip_edge_recv, land_send, land_recv, skip_send, skip_recv, out_sem,
):
    section = lax.axis_index("section")
    strip = lax.axis_index("strip")
    micro, rows, cols, channels = result.shape
    middle = sections // 2
    is_first = section == 0
    has_next = section + 1 < sections
    has_above = strip > 0
    has_below = strip + 1 < strips
    sends_skip = (section > 0) & (section < middle)
    takes_skip = section > middle
    mirror = sections - section

    weights = (
        pltpu.make_async_copy(conv_first.at[0], first_w, weight_sem.at[0]),
        pltpu.make_async_copy(conv_second.at[0], second_w, weight_sem.at[1]),
        pltpu.make_async_copy(bias_first, first_b, weight_sem.at[2]),
        pltpu.make_async_copy(bias_second, second_b, weight_sem.at[3]),
    )
    skip_weight = pltpu.make_async_copy(conv_skip.at[0], skip_w, weight_sem.at[4])
    own_rows = pltpu.make_async_copy(images, land.at[:, pl.ds(HALO, rows)], image_sem)

    even = lax.rem(strip, 2) == 0
    inner = jnp.where(even, strip + 1, strip - 1)
    outer = jnp.where(even, strip - 1, strip + 1)
    has_inner = inner < strips
    has_outer = jnp.where(even, has_above, has_below)
    half = rows // 2
    inner_row = jnp.where(even, rows - half, 0)
    outer_row = jnp.where(even, 0, rows - half)
    inner_edge = jnp.where(even, rows - HALO, 0)
    outer_edge = jnp.where(even, 0, rows - HALO)
    inner_halo = jnp.where(even, 0, HALO + rows)
    outer_halo = jnp.where(even, HALO + rows, 0)

    def halves(m):
        return [pltpu.make_async_remote_copy(
            src_ref=result.at[m, pl.ds(row, half)], dst_ref=land.at[m, pl.ds(HALO + row, half)],
            send_sem=land_send.at[m, part], recv_sem=land_recv.at[m, part],
            device_id=(section + 1, strip), device_id_type=MESH)
            for part, row in enumerate((inner_row, outer_row))]

    def edge(m, source, to_section, part):
        send = edge_send if source is result else own_send
        row, halo, to_strip = ((inner_edge, inner_halo, inner), (outer_edge, outer_halo, outer))[part]
        return pltpu.make_async_remote_copy(
            src_ref=source.at[m, pl.ds(row, HALO)], dst_ref=land.at[m, pl.ds(halo, HALO)],
            send_sem=send.at[m, part], recv_sem=edge_recv.at[m, part],
            device_id=(to_section, to_strip), device_id_type=MESH)

    def start_outer(m, source, to_section):
        @pl.when(has_outer)
        def _():
            edge(m, source, to_section, 1).start()

    def start_inner(m, source):
        @pl.when(has_inner)
        def _():
            edge(m, source, section, 0).start()

    def sent_outer(m, source):
        @pl.when(has_outer)
        def _():
            edge(m, source, section, 1).wait_send()

    def sent_inner(m):
        @pl.when(has_inner)
        def _():
            edge(m, images, section, 0).wait_send()

    def skip_edge(m, part):
        row, halo, to_strip = ((inner_edge, inner_halo, inner), (outer_edge, outer_halo, outer))[part]
        return pltpu.make_async_remote_copy(
            src_ref=skip_land.at[m, pl.ds(HALO + row, HALO)], dst_ref=skip_land.at[m, pl.ds(halo, HALO)],
            send_sem=skip_edge_send.at[m, part], recv_sem=skip_edge_recv.at[m, part],
            device_id=(section, to_strip), device_id_type=MESH)

    beside = ((has_inner, 0), (has_outer, 1))

    landed = land.at[:, pl.ds(HALO, rows)]

    def skipped(m):
        return pltpu.make_async_remote_copy(
            src_ref=land.at[m, pl.ds(HALO, rows)], dst_ref=skip_land.at[m, pl.ds(HALO, rows)],
            send_sem=skip_send.at[m], recv_sem=skip_recv.at[m],
            device_id=(mirror, strip), device_id_type=MESH)

    for copy in weights:
        copy.start()
    pl.when(section >= middle)(skip_weight.start)
    pl.when(is_first)(own_rows.start)

    barrier = pltpu.get_barrier_semaphore()

    def greet(condition, to_section, to_strip):
        @pl.when(condition)
        def _():
            pl.semaphore_signal(barrier, inc=1, device_id=(to_section, to_strip), device_id_type=MESH)

    greet(has_inner, section, inner)
    greet(has_outer, jnp.where(is_first, section, section - 1), outer)
    greet(section > 0, section - 1, strip)
    greet(takes_skip, mirror, strip)
    greet(takes_skip & has_outer, section, outer)
    inner_count, outer_count = has_inner.astype(jnp.int32), has_outer.astype(jnp.int32)
    expected = (
        inner_count
        + jnp.where(is_first | takes_skip, outer_count, 0)
        + jnp.where(has_next, outer_count + 1, 0)
        + jnp.where(sends_skip, 1, 0)
    )

    @pl.when(expected > 0)
    def _():
        pl.semaphore_wait(barrier, expected)

    @pl.when(is_first)
    def _():
        for m in range(micro):
            start_outer(m, images, section)
            start_inner(m, images)

    blank = jnp.zeros((micro, HALO, cols, channels), land.dtype)

    @pl.when(jnp.logical_not(has_above))
    def _():
        land[:, 0:HALO] = blank
        skip_land[:, 0:HALO] = blank

    @pl.when(jnp.logical_not(has_below))
    def _():
        land[:, HALO + rows:] = blank
        skip_land[:, HALO + rows:] = blank

    pl.when(section >= middle)(skip_weight.wait)
    for copy in weights:
        copy.wait()

    @pl.when(section == middle)
    def _():
        def add(tap, carry):
            total = first_w[tap].astype(jnp.float32) + skip_w[tap].astype(jnp.float32)
            first_w[tap] = total.astype(first_w.dtype)
            return carry
        lax.fori_loop(0, 9, add, 0)

    def convolve(window, weight, out_rows):
        size = out_rows * cols
        shape = (out_rows, cols, channels)
        read = jnp.concatenate([window(a).reshape(size, channels) for a in range(3)], axis=1)
        column = lax.broadcasted_iota(jnp.int32, shape, 1)

        def product(b):
            taps = jnp.concatenate([weight[3 * a + b] for a in range(3)], axis=0)
            return jnp.dot(read, taps, preferred_element_type=jnp.float32)

        def moved(value, distance, edge_column):
            rolled = pltpu.roll(value, distance % size, axis=0).reshape(shape)
            return jnp.where(column == edge_column, 0.0, rolled)

        left = moved(product(0), 1, 0)
        right = moved(product(2), -1, cols - 1)
        return left + right + product(1).reshape(shape)

    hidden_rows = rows + 2
    first_bias = first_b[...].reshape(1, 1, channels)
    second_bias = second_b[...].reshape(1, 1, channels)

    @pl.when(takes_skip)
    def _():
        for m in range(micro):
            skipped(m).wait_recv()
            for condition, part in beside:
                pl.when(condition)(skip_edge(m, part).start)

        def skip_step(m, carry):
            for condition, part in beside:
                pl.when(condition)(skip_edge(m, part).wait_recv)
            pre[m] = first_bias + convolve(
                lambda a: skip_land[m, pl.ds(a, hidden_rows)], skip_w, hidden_rows)
            return carry

        lax.fori_loop(0, micro, skip_step, 0)

    @pl.when(jnp.logical_not(takes_skip))
    def _():
        pre[...] = jnp.broadcast_to(first_bias, pre.shape)

    pl.when(is_first)(own_rows.wait)

    def hide(m, begin, count):
        hidden = convolve(lambda a: land[m, pl.ds(begin + a, count)], first_w, count)
        hidden = jnp.maximum(hidden + pre[m, pl.ds(begin, count)], 0.0)
        row = begin + lax.broadcasted_iota(jnp.int32, hidden.shape, 0)
        least = jnp.where(has_above, 0, 1)
        most = jnp.where(has_below, hidden_rows, hidden_rows - 1)
        hidden = jnp.where((row >= least) & (row < most), hidden, 0.0)
        hidden_map[pl.ds(begin, count)] = hidden.astype(jnp.bfloat16)

    def finish(m, begin):
        final = convolve(lambda a: hidden_map[pl.ds(begin + a, half)], second_w, half)
        result[m, pl.ds(begin, half)] = jnp.maximum(final + second_bias, 0.0).astype(jnp.bfloat16)

    def step(m, carry):
        @pl.when(section > 0)
        def _():
            inner_half, outer_half = halves(m)
            inner_half.wait_recv()
            start_inner(m, landed)
            outer_half.wait_recv()

        @pl.when(sends_skip)
        def _():
            skipped(m).start()

        @pl.when(has_inner)
        def _():
            edge(m, result, section, 0).wait_recv()

        inner_half, outer_half = halves(m)
        hide(m, jnp.where(even, HALO, 0), rows)
        finish(m, inner_row)
        pl.when(has_next)(inner_half.start)

        @pl.when(has_outer)
        def _():
            edge(m, result, section, 1).wait_recv()

        hide(m, jnp.where(even, 0, rows), HALO)
        finish(m, outer_row)

        @pl.when(has_next)
        def _():
            start_outer(m, result, section + 1)
            outer_half.start()

        pltpu.make_async_copy(result.at[m], out.at[0, m], out_sem.at[m]).start()
        return carry

    lax.fori_loop(0, micro, step, 0)

    for m in range(micro):
        pltpu.make_async_copy(result.at[m], out.at[0, m], out_sem.at[m]).wait()

        sent_inner(m)

        @pl.when(takes_skip)
        def _():
            for condition, part in beside:
                pl.when(condition)(skip_edge(m, part).wait_send)

        @pl.when(is_first)
        def _():
            sent_outer(m, images)

        @pl.when(has_next)
        def _():
            for copy in halves(m):
                copy.wait_send()
            sent_outer(m, result)

        @pl.when(sends_skip)
        def _():
            skipped(m).wait_send()


def body(images, conv_first, conv_skip, conv_second, bias_first, bias_second):
    sections = lax.axis_size("section")
    strips = lax.axis_size("strip")
    arguments = (images, conv_first, conv_skip, conv_second, bias_first, bias_second)
    micro, rows, cols, channels = images.shape
    padded = (micro, rows + 2 * HALO, cols, channels)
    weight = conv_first.shape[1:]
    copies = pltpu.SemaphoreType.DMA((micro, 2))
    pixels = rows * cols
    flops = 2 * micro * 2 * pixels * channels * channels * 9
    return pl.pallas_call(
        functools.partial(kernel, sections, strips),
        out_shape=jax.ShapeDtypeStruct((1, micro, rows, cols, channels), jnp.bfloat16),
        in_specs=[pl.BlockSpec(memory_space=pltpu.HBM)] * 6,
        out_specs=pl.BlockSpec(memory_space=pltpu.HBM),
        scratch_shapes=[
            pltpu.VMEM(weight, jnp.bfloat16),
            pltpu.VMEM(weight, jnp.bfloat16),
            pltpu.VMEM(weight, jnp.bfloat16),
            pltpu.VMEM((1, channels), jnp.float32),
            pltpu.VMEM((1, channels), jnp.float32),
            pltpu.VMEM(padded, jnp.bfloat16),
            pltpu.VMEM(padded, jnp.bfloat16),
            pltpu.VMEM((micro, rows, cols, channels), jnp.bfloat16),
            pltpu.VMEM((rows + 2, cols, channels), jnp.bfloat16),
            pltpu.VMEM((micro, rows + 2, cols, channels), jnp.float32),
            pltpu.SemaphoreType.DMA((5,)),
            pltpu.SemaphoreType.DMA,
            copies, copies, copies, copies, copies, copies, copies,
            pltpu.SemaphoreType.DMA((micro,)),
            pltpu.SemaphoreType.DMA((micro,)),
            pltpu.SemaphoreType.DMA((micro,)),
        ],
        compiler_params=pltpu.CompilerParams(
            collective_id=0, has_side_effects=True, vmem_limit_bytes=32 * 1024 * 1024
        ),
        cost_estimate=pl.CostEstimate(
            flops=flops, bytes_accessed=3 * conv_first.size * 2, transcendentals=0
        ),
    )(*[pltpu.with_memory_space_constraint(value, pltpu.HBM) for value in arguments])


def solution(mesh):
    placed = (
        P(None, "strip", None, None),
        P("section", None, None, None),
        P("section", None, None, None),
        P("section", None, None, None),
        P("section", None),
        P("section", None),
    )
    return jax.shard_map(
        body,
        mesh=mesh,
        in_specs=placed,
        out_specs=P("section", None, "strip", None, None),
        check_vma=False,
    )
```

```python
import functools

import jax
import jax.numpy as jnp
from jax import lax
from jax.experimental import pallas as pl
from jax.experimental.pallas import tpu as pltpu
from jax.sharding import PartitionSpec as P

MESH = pl.DeviceIdType.MESH
HALO = 2


def kernel(
    sections, strips,
    images, conv_first, conv_skip, conv_second, bias_first, bias_second,
    out,
    first_w, skip_w, second_w, first_b, second_b,
    land, skip_land, result, hidden_map, pre,
    weight_sem, image_sem, own_send, edge_send, edge_recv, skip_edge_send, skip_edge_recv, land_send, land_recv, skip_send, skip_recv, out_sem,
):
    section = lax.axis_index("section")
    strip = lax.axis_index("strip")
    micro, rows, cols, channels = result.shape
    middle = sections // 2
    is_first = section == 0
    has_next = section + 1 < sections
    has_above = strip > 0
    has_below = strip + 1 < strips
    sends_skip = (section > 0) & (section < middle)
    takes_skip = section > middle
    mirror = sections - section

    weights = (
        pltpu.make_async_copy(conv_first.at[0], first_w, weight_sem.at[0]),
        pltpu.make_async_copy(conv_second.at[0], second_w, weight_sem.at[1]),
        pltpu.make_async_copy(bias_first, first_b, weight_sem.at[2]),
        pltpu.make_async_copy(bias_second, second_b, weight_sem.at[3]),
    )
    skip_weight = pltpu.make_async_copy(conv_skip.at[0], skip_w, weight_sem.at[4])
    own_rows = pltpu.make_async_copy(images, land.at[:, pl.ds(HALO, rows)], image_sem)

    even = lax.rem(strip, 2) == 0
    inner = jnp.where(even, strip + 1, strip - 1)
    outer = jnp.where(even, strip - 1, strip + 1)
    has_inner = inner < strips
    has_outer = jnp.where(even, has_above, has_below)
    half = rows // 2
    inner_row = jnp.where(even, rows - half, 0)
    outer_row = jnp.where(even, 0, rows - half)
    inner_edge = jnp.where(even, rows - HALO, 0)
    outer_edge = jnp.where(even, 0, rows - HALO)
    inner_halo = jnp.where(even, 0, HALO + rows)
    outer_halo = jnp.where(even, HALO + rows, 0)

    landed = land.at[:, pl.ds(HALO, rows)]

    def halves(m):
        return [pltpu.make_async_remote_copy(
            src_ref=result.at[m, pl.ds(row, half)], dst_ref=land.at[m, pl.ds(HALO + row, half)],
            send_sem=land_send.at[m, part], recv_sem=land_recv.at[m, part],
            device_id=(section + 1, strip), device_id_type=MESH)
            for part, row in enumerate((inner_row, outer_row))]

    def edge(m, source, to_section, part):
        send = edge_send if source is result else own_send
        row, halo, to_strip = ((inner_edge, inner_halo, inner), (outer_edge, outer_halo, outer))[part]
        return pltpu.make_async_remote_copy(
            src_ref=source.at[m, pl.ds(row, HALO)], dst_ref=land.at[m, pl.ds(halo, HALO)],
            send_sem=send.at[m, part], recv_sem=edge_recv.at[m, part],
            device_id=(to_section, to_strip), device_id_type=MESH)

    def start_outer(m, source, to_section):
        @pl.when(has_outer)
        def _():
            edge(m, source, to_section, 1).start()

    def start_inner(m):
        @pl.when(has_inner)
        def _():
            edge(m, landed, section, 0).start()

    def sent_outer(m, source):
        @pl.when(has_outer)
        def _():
            edge(m, source, section, 1).wait_send()

    def sent_inner(m):
        @pl.when(has_inner)
        def _():
            edge(m, landed, section, 0).wait_send()

    def skip_edge(m, part):
        row, halo, to_strip = ((inner_edge, inner_halo, inner), (outer_edge, outer_halo, outer))[part]
        return pltpu.make_async_remote_copy(
            src_ref=skip_land.at[m, pl.ds(HALO + row, HALO)], dst_ref=skip_land.at[m, pl.ds(halo, HALO)],
            send_sem=skip_edge_send.at[m, part], recv_sem=skip_edge_recv.at[m, part],
            device_id=(section, to_strip), device_id_type=MESH)

    beside = ((has_inner, 0), (has_outer, 1))

    def skipped(m):
        return pltpu.make_async_remote_copy(
            src_ref=land.at[m, pl.ds(HALO, rows)], dst_ref=skip_land.at[m, pl.ds(HALO, rows)],
            send_sem=skip_send.at[m], recv_sem=skip_recv.at[m],
            device_id=(mirror, strip), device_id_type=MESH)

    pl.when(is_first)(own_rows.start)
    for copy in weights:
        copy.start()
    pl.when(section >= middle)(skip_weight.start)

    barrier = pltpu.get_barrier_semaphore()

    def greet(condition, to_section, to_strip):
        @pl.when(condition)
        def _():
            pl.semaphore_signal(barrier, inc=1, device_id=(to_section, to_strip), device_id_type=MESH)

    greet(has_inner, section, inner)
    greet(has_outer, jnp.where(is_first, section, section - 1), outer)
    greet(section > 0, section - 1, strip)
    greet(takes_skip, mirror, strip)
    greet(takes_skip & has_outer, section, outer)
    inner_count, outer_count = has_inner.astype(jnp.int32), has_outer.astype(jnp.int32)
    expected = (
        inner_count
        + jnp.where(is_first | takes_skip, outer_count, 0)
        + jnp.where(has_next, outer_count + 1, 0)
        + jnp.where(sends_skip, 1, 0)
    )

    @pl.when(expected > 0)
    def _():
        pl.semaphore_wait(barrier, expected)

    @pl.when(is_first)
    def _():
        own_rows.wait()
        for m in range(micro):
            start_outer(m, landed, section)
            start_inner(m)

    blank = jnp.zeros((micro, HALO, cols, channels), land.dtype)

    @pl.when(jnp.logical_not(has_above))
    def _():
        land[:, 0:HALO] = blank
        skip_land[:, 0:HALO] = blank

    @pl.when(jnp.logical_not(has_below))
    def _():
        land[:, HALO + rows:] = blank
        skip_land[:, HALO + rows:] = blank

    pl.when(section >= middle)(skip_weight.wait)
    for copy in weights:
        copy.wait()

    @pl.when(section == middle)
    def _():
        def add(tap, carry):
            total = first_w[tap].astype(jnp.float32) + skip_w[tap].astype(jnp.float32)
            first_w[tap] = total.astype(first_w.dtype)
            return carry
        lax.fori_loop(0, 9, add, 0)

    def convolve(window, weight, out_rows):
        size = out_rows * cols
        shape = (out_rows, cols, channels)
        read = jnp.concatenate([window(a).reshape(size, channels) for a in range(3)], axis=1)
        column = lax.broadcasted_iota(jnp.int32, shape, 1)

        def product(b):
            taps = jnp.concatenate([weight[3 * a + b] for a in range(3)], axis=0)
            return jnp.dot(read, taps, preferred_element_type=jnp.float32)

        def moved(value, distance, edge_column):
            rolled = pltpu.roll(value, distance % size, axis=0).reshape(shape)
            return jnp.where(column == edge_column, 0.0, rolled)

        left = moved(product(0), 1, 0)
        right = moved(product(2), -1, cols - 1)
        return left + right + product(1).reshape(shape)

    hidden_rows = rows + 2
    first_bias = first_b[...].reshape(1, 1, channels)
    second_bias = second_b[...].reshape(1, 1, channels)

    @pl.when(takes_skip)
    def _():
        for m in range(micro):
            skipped(m).wait_recv()
            for condition, part in beside:
                pl.when(condition)(skip_edge(m, part).start)

        def skip_step(m, carry):
            for condition, part in beside:
                pl.when(condition)(skip_edge(m, part).wait_recv)
            pre[m] = first_bias + convolve(
                lambda a: skip_land[m, pl.ds(a, hidden_rows)], skip_w, hidden_rows)
            return carry

        lax.fori_loop(0, micro, skip_step, 0)

    @pl.when(jnp.logical_not(takes_skip))
    def _():
        pre[...] = jnp.broadcast_to(first_bias, pre.shape)


    def hide(m, begin, count):
        hidden = convolve(lambda a: land[m, pl.ds(begin + a, count)], first_w, count)
        hidden = jnp.maximum(hidden + pre[m, pl.ds(begin, count)], 0.0)
        row = begin + lax.broadcasted_iota(jnp.int32, hidden.shape, 0)
        least = jnp.where(has_above, 0, 1)
        most = jnp.where(has_below, hidden_rows, hidden_rows - 1)
        hidden = jnp.where((row >= least) & (row < most), hidden, 0.0)
        hidden_map[m, pl.ds(begin, count)] = hidden.astype(jnp.bfloat16)

    def finish(m, begin):
        final = convolve(lambda a: hidden_map[m, pl.ds(begin + a, half)], second_w, half)
        result[m, pl.ds(begin, half)] = jnp.maximum(final + second_bias, 0.0).astype(jnp.bfloat16)

    def inside(m, carry=0):
        @pl.when(has_inner)
        def _():
            edge(m, landed, section, 0).wait_recv()

        hide(m, jnp.where(even, HALO, 0), rows)
        finish(m, inner_row)
        pl.when(has_next)(halves(m)[0].start)
        return carry

    @pl.when(is_first)
    def _():
        lax.fori_loop(0, micro, inside, 0)

    def step(m, carry):
        @pl.when(section > 0)
        def _():
            inner_half, outer_half = halves(m)
            inner_half.wait_recv()
            start_inner(m)
            outer_half.wait_recv()
            pl.when(sends_skip)(skipped(m).start)
            inside(m)

        outer_half = halves(m)[1]

        @pl.when(has_outer)
        def _():
            edge(m, result, section, 1).wait_recv()

        hide(m, jnp.where(even, 0, rows), HALO)
        finish(m, outer_row)

        @pl.when(has_next)
        def _():
            outer_half.start()
            start_outer(m, result, section + 1)

        pltpu.make_async_copy(result.at[m], out.at[0, m], out_sem.at[m]).start()
        return carry

    lax.fori_loop(0, micro, step, 0)

    for m in range(micro):
        pltpu.make_async_copy(result.at[m], out.at[0, m], out_sem.at[m]).wait()

        sent_inner(m)

        @pl.when(takes_skip)
        def _():
            for condition, part in beside:
                pl.when(condition)(skip_edge(m, part).wait_send)

        @pl.when(is_first)
        def _():
            sent_outer(m, landed)

        @pl.when(has_next)
        def _():
            for copy in halves(m):
                copy.wait_send()
            sent_outer(m, result)

        @pl.when(sends_skip)
        def _():
            skipped(m).wait_send()


def body(images, conv_first, conv_skip, conv_second, bias_first, bias_second):
    sections = lax.axis_size("section")
    strips = lax.axis_size("strip")
    arguments = (images, conv_first, conv_skip, conv_second, bias_first, bias_second)
    micro, rows, cols, channels = images.shape
    padded = (micro, rows + 2 * HALO, cols, channels)
    weight = conv_first.shape[1:]
    copies = pltpu.SemaphoreType.DMA((micro, 2))
    pixels = rows * cols
    flops = 2 * micro * 2 * pixels * channels * channels * 9
    return pl.pallas_call(
        functools.partial(kernel, sections, strips),
        out_shape=jax.ShapeDtypeStruct((1, micro, rows, cols, channels), jnp.bfloat16),
        in_specs=[pl.BlockSpec(memory_space=pltpu.HBM)] * 6,
        out_specs=pl.BlockSpec(memory_space=pltpu.HBM),
        scratch_shapes=[
            pltpu.VMEM(weight, jnp.bfloat16),
            pltpu.VMEM(weight, jnp.bfloat16),
            pltpu.VMEM(weight, jnp.bfloat16),
            pltpu.VMEM((1, channels), jnp.float32),
            pltpu.VMEM((1, channels), jnp.float32),
            pltpu.VMEM(padded, jnp.bfloat16),
            pltpu.VMEM(padded, jnp.bfloat16),
            pltpu.VMEM((micro, rows, cols, channels), jnp.bfloat16),
            pltpu.VMEM((micro, rows + 2, cols, channels), jnp.bfloat16),
            pltpu.VMEM((micro, rows + 2, cols, channels), jnp.float32),
            pltpu.SemaphoreType.DMA((5,)),
            pltpu.SemaphoreType.DMA,
            copies, copies, copies, copies, copies, copies, copies,
            pltpu.SemaphoreType.DMA((micro,)),
            pltpu.SemaphoreType.DMA((micro,)),
            pltpu.SemaphoreType.DMA((micro,)),
        ],
        compiler_params=pltpu.CompilerParams(
            collective_id=0, has_side_effects=True, vmem_limit_bytes=32 * 1024 * 1024
        ),
        cost_estimate=pl.CostEstimate(
            flops=flops, bytes_accessed=3 * conv_first.size * 2, transcendentals=0
        ),
    )(*[pltpu.with_memory_space_constraint(value, pltpu.HBM) for value in arguments])


def solution(mesh):
    placed = (
        P(None, "strip", None, None),
        P("section", None, None, None),
        P("section", None, None, None),
        P("section", None, None, None),
        P("section", None),
        P("section", None),
    )
    return jax.shard_map(
        body,
        mesh=mesh,
        in_specs=placed,
        out_specs=P("section", None, "strip", None, None),
        check_vma=False,
    )
```

```python
import functools

import jax
import jax.numpy as jnp
from jax import lax
from jax.experimental import pallas as pl
from jax.experimental.pallas import tpu as pltpu
from jax.sharding import PartitionSpec as P

MESH = pl.DeviceIdType.MESH
HALO = 2


def kernel(
    sections, strips,
    images, conv_first, conv_skip, conv_second, bias_first, bias_second,
    out,
    first_w, skip_w, second_w, first_b, second_b,
    land, skip_land, result, hidden_map, pre,
    weight_sem, image_sem, own_send, edge_send, edge_recv, skip_edge_send, skip_edge_recv, land_send, land_recv, skip_send, skip_recv, out_sem,
):
    section = lax.axis_index("section")
    strip = lax.axis_index("strip")
    micro, rows, cols, channels = result.shape
    middle = sections // 2
    is_first = section == 0
    has_next = section + 1 < sections
    has_above = strip > 0
    has_below = strip + 1 < strips
    sends_skip = (section > 0) & (section < middle)
    takes_skip = section > middle
    mirror = sections - section

    weights = (
        pltpu.make_async_copy(conv_first.at[0], first_w, weight_sem.at[0]),
        pltpu.make_async_copy(conv_second.at[0], second_w, weight_sem.at[1]),
        pltpu.make_async_copy(bias_first, first_b, weight_sem.at[2]),
        pltpu.make_async_copy(bias_second, second_b, weight_sem.at[3]),
    )
    skip_weight = pltpu.make_async_copy(conv_skip.at[0], skip_w, weight_sem.at[4])
    own_rows = pltpu.make_async_copy(images, land.at[:, pl.ds(HALO, rows)], image_sem)

    even = lax.rem(strip, 2) == 0
    inner = jnp.where(even, strip + 1, strip - 1)
    outer = jnp.where(even, strip - 1, strip + 1)
    has_inner = inner < strips
    has_outer = jnp.where(even, has_above, has_below)
    half = rows // 2
    inner_row = jnp.where(even, rows - half, 0)
    outer_row = jnp.where(even, 0, rows - half)
    inner_edge = jnp.where(even, rows - HALO, 0)
    outer_edge = jnp.where(even, 0, rows - HALO)
    inner_halo = jnp.where(even, 0, HALO + rows)
    outer_halo = jnp.where(even, HALO + rows, 0)

    landed = land.at[:, pl.ds(HALO, rows)]

    def halves(m):
        return [pltpu.make_async_remote_copy(
            src_ref=result.at[m, pl.ds(row, half)], dst_ref=land.at[m, pl.ds(HALO + row, half)],
            send_sem=land_send.at[m, part], recv_sem=land_recv.at[m, part],
            device_id=(section + 1, strip), device_id_type=MESH)
            for part, row in enumerate((inner_row, outer_row))]

    def edge(m, source, to_section, part):
        send = edge_send if source is result else own_send
        row, halo, to_strip = ((inner_edge, inner_halo, inner), (outer_edge, outer_halo, outer))[part]
        return pltpu.make_async_remote_copy(
            src_ref=source.at[m, pl.ds(row, HALO)], dst_ref=land.at[m, pl.ds(halo, HALO)],
            send_sem=send.at[m, part], recv_sem=edge_recv.at[m, part],
            device_id=(to_section, to_strip), device_id_type=MESH)

    def start_outer(m, source, to_section):
        @pl.when(has_outer)
        def _():
            edge(m, source, to_section, 1).start()

    def start_inner(m):
        @pl.when(has_inner)
        def _():
            edge(m, landed, section, 0).start()

    def sent_outer(m, source):
        @pl.when(has_outer)
        def _():
            edge(m, source, section, 1).wait_send()

    def sent_inner(m):
        @pl.when(has_inner)
        def _():
            edge(m, landed, section, 0).wait_send()

    def skip_edge(m, part):
        row, halo, to_strip = ((inner_edge, inner_halo, inner), (outer_edge, outer_halo, outer))[part]
        return pltpu.make_async_remote_copy(
            src_ref=skip_land.at[m, pl.ds(HALO + row, HALO)], dst_ref=skip_land.at[m, pl.ds(halo, HALO)],
            send_sem=skip_edge_send.at[m, part], recv_sem=skip_edge_recv.at[m, part],
            device_id=(section, to_strip), device_id_type=MESH)

    beside = ((has_inner, 0), (has_outer, 1))

    def skipped(m):
        return pltpu.make_async_remote_copy(
            src_ref=land.at[m, pl.ds(HALO, rows)], dst_ref=skip_land.at[m, pl.ds(HALO, rows)],
            send_sem=skip_send.at[m], recv_sem=skip_recv.at[m],
            device_id=(mirror, strip), device_id_type=MESH)

    pl.when(is_first)(own_rows.start)
    for copy in weights:
        copy.start()
    pl.when(section >= middle)(skip_weight.start)

    barrier = pltpu.get_barrier_semaphore()

    def greet(condition, to_section, to_strip):
        @pl.when(condition)
        def _():
            pl.semaphore_signal(barrier, inc=1, device_id=(to_section, to_strip), device_id_type=MESH)

    greet(has_inner, section, inner)
    greet(has_outer, jnp.where(is_first, section, section - 1), outer)
    greet(section > 0, section - 1, strip)
    greet(takes_skip, mirror, strip)
    greet(takes_skip & has_outer, section, outer)
    inner_count, outer_count = has_inner.astype(jnp.int32), has_outer.astype(jnp.int32)
    expected = (
        inner_count
        + jnp.where(is_first | takes_skip, outer_count, 0)
        + jnp.where(has_next, outer_count + 1, 0)
        + jnp.where(sends_skip, 1, 0)
    )

    @pl.when(expected > 0)
    def _():
        pl.semaphore_wait(barrier, expected)

    @pl.when(is_first)
    def _():
        own_rows.wait()
        for m in range(micro):
            start_outer(m, landed, section)
            start_inner(m)

    blank = jnp.zeros((micro, HALO, cols, channels), land.dtype)

    @pl.when(jnp.logical_not(has_above))
    def _():
        land[:, 0:HALO] = blank
        skip_land[:, 0:HALO] = blank

    @pl.when(jnp.logical_not(has_below))
    def _():
        land[:, HALO + rows:] = blank
        skip_land[:, HALO + rows:] = blank

    pl.when(section >= middle)(skip_weight.wait)
    for copy in weights:
        copy.wait()

    @pl.when(section == middle)
    def _():
        def add(tap, carry):
            total = first_w[tap].astype(jnp.float32) + skip_w[tap].astype(jnp.float32)
            first_w[tap] = total.astype(first_w.dtype)
            return carry
        lax.fori_loop(0, 9, add, 0)

    def convolve(window, weight, out_rows):
        size = out_rows * cols
        shape = (out_rows, cols, channels)
        read = jnp.concatenate([window(a).reshape(size, channels) for a in range(3)], axis=1)
        column = lax.broadcasted_iota(jnp.int32, shape, 1)

        def product(b):
            taps = jnp.concatenate([weight[3 * a + b] for a in range(3)], axis=0)
            return jnp.dot(read, taps, preferred_element_type=jnp.float32)

        def moved(value, distance, edge_column):
            rolled = pltpu.roll(value, distance % size, axis=0).reshape(shape)
            return jnp.where(column == edge_column, 0.0, rolled)

        left = moved(product(0), 1, 0)
        right = moved(product(2), -1, cols - 1)
        return left + right + product(1).reshape(shape)

    hidden_rows = rows + 2
    first_bias = first_b[...].reshape(1, 1, channels)
    second_bias = second_b[...].reshape(1, 1, channels)

    @pl.when(takes_skip)
    def _():
        for m in range(micro):
            skipped(m).wait_recv()
            for condition, part in beside:
                pl.when(condition)(skip_edge(m, part).start)

        def skip_step(m, carry):
            for condition, part in beside:
                pl.when(condition)(skip_edge(m, part).wait_recv)
            pre[m] = first_bias + convolve(
                lambda a: skip_land[m, pl.ds(a, hidden_rows)], skip_w, hidden_rows)
            return carry

        lax.fori_loop(0, micro, skip_step, 0)

    @pl.when(jnp.logical_not(takes_skip))
    def _():
        pre[...] = jnp.broadcast_to(first_bias, pre.shape)


    def hide(m, begin, count):
        hidden = convolve(lambda a: land[m, pl.ds(begin + a, count)], first_w, count)
        hidden = jnp.maximum(hidden + pre[m, pl.ds(begin, count)], 0.0)
        row = begin + lax.broadcasted_iota(jnp.int32, hidden.shape, 0)
        least = jnp.where(has_above, 0, 1)
        most = jnp.where(has_below, hidden_rows, hidden_rows - 1)
        hidden = jnp.where((row >= least) & (row < most), hidden, 0.0)
        hidden_map[m, pl.ds(begin, count)] = hidden.astype(jnp.bfloat16)

    def finish(m, begin):
        final = convolve(lambda a: hidden_map[m, pl.ds(begin + a, half)], second_w, half)
        result[m, pl.ds(begin, half)] = jnp.maximum(final + second_bias, 0.0).astype(jnp.bfloat16)

    def inside(m, carry=0):
        @pl.when(has_inner)
        def _():
            edge(m, landed, section, 0).wait_recv()

        hide(m, jnp.where(even, HALO, 0), rows)
        finish(m, inner_row)
        pl.when(has_next)(halves(m)[0].start)
        return carry

    @pl.when(is_first)
    def _():
        lax.fori_loop(0, micro, inside, 0)

    def step(m, carry):
        @pl.when(section > 0)
        def _():
            inner_half, outer_half = halves(m)
            inner_half.wait_recv()
            start_inner(m)
            outer_half.wait_recv()
            pl.when(sends_skip)(skipped(m).start)
            inside(m)

        outer_half = halves(m)[1]

        @pl.when(has_outer)
        def _():
            edge(m, result, section, 1).wait_recv()

        hide(m, jnp.where(even, 0, rows), HALO)
        finish(m, outer_row)

        @pl.when(has_next)
        def _():
            start_outer(m, result, section + 1)
            outer_half.start()

        pltpu.make_async_copy(result.at[m], out.at[0, m], out_sem.at[m]).start()
        return carry

    lax.fori_loop(0, micro, step, 0)

    for m in range(micro):
        pltpu.make_async_copy(result.at[m], out.at[0, m], out_sem.at[m]).wait()

        sent_inner(m)

        @pl.when(takes_skip)
        def _():
            for condition, part in beside:
                pl.when(condition)(skip_edge(m, part).wait_send)

        @pl.when(is_first)
        def _():
            sent_outer(m, landed)

        @pl.when(has_next)
        def _():
            for copy in halves(m):
                copy.wait_send()
            sent_outer(m, result)

        @pl.when(sends_skip)
        def _():
            skipped(m).wait_send()


def body(images, conv_first, conv_skip, conv_second, bias_first, bias_second):
    sections = lax.axis_size("section")
    strips = lax.axis_size("strip")
    arguments = (images, conv_first, conv_skip, conv_second, bias_first, bias_second)
    micro, rows, cols, channels = images.shape
    padded = (micro, rows + 2 * HALO, cols, channels)
    weight = conv_first.shape[1:]
    copies = pltpu.SemaphoreType.DMA((micro, 2))
    pixels = rows * cols
    flops = 2 * micro * 2 * pixels * channels * channels * 9
    return pl.pallas_call(
        functools.partial(kernel, sections, strips),
        out_shape=jax.ShapeDtypeStruct((1, micro, rows, cols, channels), jnp.bfloat16),
        in_specs=[pl.BlockSpec(memory_space=pltpu.HBM)] * 6,
        out_specs=pl.BlockSpec(memory_space=pltpu.HBM),
        scratch_shapes=[
            pltpu.VMEM(weight, jnp.bfloat16),
            pltpu.VMEM(weight, jnp.bfloat16),
            pltpu.VMEM(weight, jnp.bfloat16),
            pltpu.VMEM((1, channels), jnp.float32),
            pltpu.VMEM((1, channels), jnp.float32),
            pltpu.VMEM(padded, jnp.bfloat16),
            pltpu.VMEM(padded, jnp.bfloat16),
            pltpu.VMEM((micro, rows, cols, channels), jnp.bfloat16),
            pltpu.VMEM((micro, rows + 2, cols, channels), jnp.bfloat16),
            pltpu.VMEM((micro, rows + 2, cols, channels), jnp.float32),
            pltpu.SemaphoreType.DMA((5,)),
            pltpu.SemaphoreType.DMA,
            copies, copies, copies, copies, copies, copies, copies,
            pltpu.SemaphoreType.DMA((micro,)),
            pltpu.SemaphoreType.DMA((micro,)),
            pltpu.SemaphoreType.DMA((micro,)),
        ],
        compiler_params=pltpu.CompilerParams(
            collective_id=0, has_side_effects=True, vmem_limit_bytes=32 * 1024 * 1024
        ),
        cost_estimate=pl.CostEstimate(
            flops=flops, bytes_accessed=3 * conv_first.size * 2, transcendentals=0
        ),
    )(*[pltpu.with_memory_space_constraint(value, pltpu.HBM) for value in arguments])


def solution(mesh):
    placed = (
        P(None, "strip", None, None),
        P("section", None, None, None),
        P("section", None, None, None),
        P("section", None, None, None),
        P("section", None),
        P("section", None),
    )
    return jax.shard_map(
        body,
        mesh=mesh,
        in_specs=placed,
        out_specs=P("section", None, "strip", None, None),
        check_vma=False,
    )
```

```python
import functools

import jax
import jax.numpy as jnp
from jax import lax
from jax.experimental import pallas as pl
from jax.experimental.pallas import tpu as pltpu
from jax.sharding import PartitionSpec as P

MESH = pl.DeviceIdType.MESH
HALO = 2


def kernel(
    sections, strips,
    images, conv_first, conv_skip, conv_second, bias_first, bias_second,
    out,
    first_w, skip_w, second_w, first_b, second_b,
    land, skip_land, result, hidden_map, pre,
    weight_sem, image_sem, own_send, edge_send, edge_recv, skip_edge_send, skip_edge_recv, land_send, land_recv, skip_send, skip_recv, out_sem,
):
    section = lax.axis_index("section")
    strip = lax.axis_index("strip")
    micro, rows, cols, channels = result.shape
    middle = sections // 2
    is_first = section == 0
    has_next = section + 1 < sections
    has_above = strip > 0
    has_below = strip + 1 < strips
    sends_skip = (section > 0) & (section < middle)
    takes_skip = section > middle
    mirror = sections - section

    weights = (
        pltpu.make_async_copy(conv_first.at[0], first_w, weight_sem.at[0]),
        pltpu.make_async_copy(conv_second.at[0], second_w, weight_sem.at[1]),
        pltpu.make_async_copy(bias_first, first_b, weight_sem.at[2]),
        pltpu.make_async_copy(bias_second, second_b, weight_sem.at[3]),
    )
    skip_weight = pltpu.make_async_copy(conv_skip.at[0], skip_w, weight_sem.at[4])
    own_rows = pltpu.make_async_copy(images, land.at[:, pl.ds(HALO, rows)], image_sem)

    even = lax.rem(strip, 2) == 0
    inner = jnp.where(even, strip + 1, strip - 1)
    outer = jnp.where(even, strip - 1, strip + 1)
    has_inner = inner < strips
    has_outer = jnp.where(even, has_above, has_below)
    half = rows // 2
    inner_row = jnp.where(even, rows - half, 0)
    outer_row = jnp.where(even, 0, rows - half)
    inner_edge = jnp.where(even, rows - HALO, 0)
    outer_edge = jnp.where(even, 0, rows - HALO)
    inner_halo = jnp.where(even, 0, HALO + rows)
    outer_halo = jnp.where(even, HALO + rows, 0)

    landed = land.at[:, pl.ds(HALO, rows)]

    def halves(m):
        return [pltpu.make_async_remote_copy(
            src_ref=result.at[m, pl.ds(row, half)], dst_ref=land.at[m, pl.ds(HALO + row, half)],
            send_sem=land_send.at[m, part], recv_sem=land_recv.at[m, part],
            device_id=(section + 1, strip), device_id_type=MESH)
            for part, row in enumerate((inner_row, outer_row))]

    def edge(m, source, to_section, part):
        send = edge_send if source is result else own_send
        row, halo, to_strip = ((inner_edge, inner_halo, inner), (outer_edge, outer_halo, outer))[part]
        return pltpu.make_async_remote_copy(
            src_ref=source.at[m, pl.ds(row, HALO)], dst_ref=land.at[m, pl.ds(halo, HALO)],
            send_sem=send.at[m, part], recv_sem=edge_recv.at[m, part],
            device_id=(to_section, to_strip), device_id_type=MESH)

    def start_outer(m, source, to_section):
        @pl.when(has_outer)
        def _():
            edge(m, source, to_section, 1).start()

    def start_inner(m):
        @pl.when(has_inner)
        def _():
            edge(m, landed, section, 0).start()

    def sent_outer(m, source):
        @pl.when(has_outer)
        def _():
            edge(m, source, section, 1).wait_send()

    def sent_inner(m):
        @pl.when(has_inner)
        def _():
            edge(m, landed, section, 0).wait_send()

    def skip_edge(m, part):
        row, halo, to_strip = ((inner_edge, inner_halo, inner), (outer_edge, outer_halo, outer))[part]
        return pltpu.make_async_remote_copy(
            src_ref=skip_land.at[m, pl.ds(HALO + row, HALO)], dst_ref=skip_land.at[m, pl.ds(halo, HALO)],
            send_sem=skip_edge_send.at[m, part], recv_sem=skip_edge_recv.at[m, part],
            device_id=(section, to_strip), device_id_type=MESH)

    beside = ((has_inner, 0), (has_outer, 1))

    def written(m):
        return [pltpu.make_async_copy(
            result.at[m, pl.ds(row, half)], out.at[0, m, pl.ds(row, half)], out_sem.at[m, part])
            for part, row in enumerate((inner_row, outer_row))]

    def skipped(m):
        return pltpu.make_async_remote_copy(
            src_ref=land.at[m, pl.ds(HALO, rows)], dst_ref=skip_land.at[m, pl.ds(HALO, rows)],
            send_sem=skip_send.at[m], recv_sem=skip_recv.at[m],
            device_id=(mirror, strip), device_id_type=MESH)

    pl.when(is_first)(own_rows.start)
    for copy in weights:
        copy.start()
    pl.when(section >= middle)(skip_weight.start)

    barrier = pltpu.get_barrier_semaphore()

    def greet(condition, to_section, to_strip):
        @pl.when(condition)
        def _():
            pl.semaphore_signal(barrier, inc=1, device_id=(to_section, to_strip), device_id_type=MESH)

    greet(has_inner, section, inner)
    greet(has_outer, jnp.where(is_first, section, section - 1), outer)
    greet(section > 0, section - 1, strip)
    greet(takes_skip, mirror, strip)
    greet(takes_skip & has_outer, section, outer)
    inner_count, outer_count = has_inner.astype(jnp.int32), has_outer.astype(jnp.int32)
    expected = (
        inner_count
        + jnp.where(is_first | takes_skip, outer_count, 0)
        + jnp.where(has_next, outer_count + 1, 0)
        + jnp.where(sends_skip, 1, 0)
    )

    @pl.when(expected > 0)
    def _():
        pl.semaphore_wait(barrier, expected)

    @pl.when(is_first)
    def _():
        own_rows.wait()
        for m in range(micro):
            start_outer(m, landed, section)
        for m in range(micro):
            start_inner(m)

    blank = jnp.zeros((micro, HALO, cols, channels), land.dtype)

    @pl.when(jnp.logical_not(has_above))
    def _():
        land[:, 0:HALO] = blank
        skip_land[:, 0:HALO] = blank

    @pl.when(jnp.logical_not(has_below))
    def _():
        land[:, HALO + rows:] = blank
        skip_land[:, HALO + rows:] = blank

    pl.when(section >= middle)(skip_weight.wait)
    for copy in weights:
        copy.wait()

    @pl.when(section == middle)
    def _():
        def add(tap, carry):
            total = first_w[tap].astype(jnp.float32) + skip_w[tap].astype(jnp.float32)
            first_w[tap] = total.astype(first_w.dtype)
            return carry
        lax.fori_loop(0, 9, add, 0)

    def convolve(window, weight, out_rows):
        size = out_rows * cols
        shape = (out_rows, cols, channels)
        read = jnp.concatenate([window(a).reshape(size, channels) for a in range(3)], axis=1)
        column = lax.broadcasted_iota(jnp.int32, shape, 1)

        def product(b):
            taps = jnp.concatenate([weight[3 * a + b] for a in range(3)], axis=0)
            return jnp.dot(read, taps, preferred_element_type=jnp.float32)

        def moved(value, distance, edge_column):
            rolled = pltpu.roll(value, distance % size, axis=0).reshape(shape)
            return jnp.where(column == edge_column, 0.0, rolled)

        left = moved(product(0), 1, 0)
        right = moved(product(2), -1, cols - 1)
        return left + right + product(1).reshape(shape)

    hidden_rows = rows + 2
    first_bias = first_b[...].reshape(1, 1, channels)
    second_bias = second_b[...].reshape(1, 1, channels)

    @pl.when(takes_skip)
    def _():
        for m in range(micro):
            skipped(m).wait_recv()
            for condition, part in beside:
                pl.when(condition)(skip_edge(m, part).start)

        def skip_step(m, carry):
            for condition, part in beside:
                pl.when(condition)(skip_edge(m, part).wait_recv)
            pre[m] = first_bias + convolve(
                lambda a: skip_land[m, pl.ds(a, hidden_rows)], skip_w, hidden_rows)
            return carry

        lax.fori_loop(0, micro, skip_step, 0)

    @pl.when(jnp.logical_not(takes_skip))
    def _():
        pre[...] = jnp.broadcast_to(first_bias, pre.shape)


    def hide(m, begin, count):
        hidden = convolve(lambda a: land[m, pl.ds(begin + a, count)], first_w, count)
        hidden = jnp.maximum(hidden + pre[m, pl.ds(begin, count)], 0.0)
        row = begin + lax.broadcasted_iota(jnp.int32, hidden.shape, 0)
        least = jnp.where(has_above, 0, 1)
        most = jnp.where(has_below, hidden_rows, hidden_rows - 1)
        hidden = jnp.where((row >= least) & (row < most), hidden, 0.0)
        hidden_map[pl.ds(begin, count)] = hidden.astype(jnp.bfloat16)

    def finish(m, begin):
        final = convolve(lambda a: hidden_map[pl.ds(begin + a, half)], second_w, half)
        result[m, pl.ds(begin, half)] = jnp.maximum(final + second_bias, 0.0).astype(jnp.bfloat16)

    def step(m, carry):
        @pl.when(section > 0)
        def _():
            inner_half, outer_half = halves(m)
            inner_half.wait_recv()
            start_inner(m)
            outer_half.wait_recv()

        @pl.when(sends_skip)
        def _():
            skipped(m).start()

        @pl.when(has_inner)
        def _():
            edge(m, result, section, 0).wait_recv()

        inner_half, outer_half = halves(m)
        hide(m, jnp.where(even, HALO, 0), rows)
        finish(m, inner_row)
        pl.when(has_next)(inner_half.start)
        written(m)[0].start()

        @pl.when(has_outer)
        def _():
            edge(m, result, section, 1).wait_recv()

        hide(m, jnp.where(even, 0, rows), HALO)
        finish(m, outer_row)

        @pl.when(has_next)
        def _():
            start_outer(m, result, section + 1)
            outer_half.start()

        written(m)[1].start()
        return carry

    lax.fori_loop(0, micro, step, 0)

    for m in range(micro):
        for copy in written(m):
            copy.wait()

        sent_inner(m)

        @pl.when(takes_skip)
        def _():
            for condition, part in beside:
                pl.when(condition)(skip_edge(m, part).wait_send)

        @pl.when(is_first)
        def _():
            sent_outer(m, landed)

        @pl.when(has_next)
        def _():
            for copy in halves(m):
                copy.wait_send()
            sent_outer(m, result)

        @pl.when(sends_skip)
        def _():
            skipped(m).wait_send()


def body(images, conv_first, conv_skip, conv_second, bias_first, bias_second):
    sections = lax.axis_size("section")
    strips = lax.axis_size("strip")
    arguments = (images, conv_first, conv_skip, conv_second, bias_first, bias_second)
    micro, rows, cols, channels = images.shape
    padded = (micro, rows + 2 * HALO, cols, channels)
    weight = conv_first.shape[1:]
    copies = pltpu.SemaphoreType.DMA((micro, 2))
    pixels = rows * cols
    flops = 2 * micro * 2 * pixels * channels * channels * 9
    return pl.pallas_call(
        functools.partial(kernel, sections, strips),
        out_shape=jax.ShapeDtypeStruct((1, micro, rows, cols, channels), jnp.bfloat16),
        in_specs=[pl.BlockSpec(memory_space=pltpu.HBM)] * 6,
        out_specs=pl.BlockSpec(memory_space=pltpu.HBM),
        scratch_shapes=[
            pltpu.VMEM(weight, jnp.bfloat16),
            pltpu.VMEM(weight, jnp.bfloat16),
            pltpu.VMEM(weight, jnp.bfloat16),
            pltpu.VMEM((1, channels), jnp.float32),
            pltpu.VMEM((1, channels), jnp.float32),
            pltpu.VMEM(padded, jnp.bfloat16),
            pltpu.VMEM(padded, jnp.bfloat16),
            pltpu.VMEM((micro, rows, cols, channels), jnp.bfloat16),
            pltpu.VMEM((rows + 2, cols, channels), jnp.bfloat16),
            pltpu.VMEM((micro, rows + 2, cols, channels), jnp.float32),
            pltpu.SemaphoreType.DMA((5,)),
            pltpu.SemaphoreType.DMA,
            copies, copies, copies, copies, copies, copies, copies,
            pltpu.SemaphoreType.DMA((micro,)),
            pltpu.SemaphoreType.DMA((micro,)),
            copies,
        ],
        compiler_params=pltpu.CompilerParams(
            collective_id=0, has_side_effects=True, vmem_limit_bytes=32 * 1024 * 1024
        ),
        cost_estimate=pl.CostEstimate(
            flops=flops, bytes_accessed=3 * conv_first.size * 2, transcendentals=0
        ),
    )(*[pltpu.with_memory_space_constraint(value, pltpu.HBM) for value in arguments])


def solution(mesh):
    placed = (
        P(None, "strip", None, None),
        P("section", None, None, None),
        P("section", None, None, None),
        P("section", None, None, None),
        P("section", None),
        P("section", None),
    )
    return jax.shard_map(
        body,
        mesh=mesh,
        in_specs=placed,
        out_specs=P("section", None, "strip", None, None),
        check_vma=False,
    )
```

```python
import functools

import jax
import jax.numpy as jnp
from jax import lax
from jax.experimental import pallas as pl
from jax.experimental.pallas import tpu as pltpu
from jax.sharding import PartitionSpec as P

MESH = pl.DeviceIdType.MESH
HALO = 2


def kernel(
    sections, strips,
    images, conv_first, conv_skip, conv_second, bias_first, bias_second,
    out,
    first_w, skip_w, second_w, first_b, second_b,
    land, skip_land, result, hidden_map, pre,
    weight_sem, image_sem, own_send, edge_send, edge_recv, skip_edge_send, skip_edge_recv, land_send, land_recv, skip_send, skip_recv, out_sem,
):
    section = lax.axis_index("section")
    strip = lax.axis_index("strip")
    micro, rows, cols, channels = result.shape
    middle = sections // 2
    is_first = section == 0
    has_next = section + 1 < sections
    has_above = strip > 0
    has_below = strip + 1 < strips
    sends_skip = (section > 0) & (section < middle)
    takes_skip = section > middle
    mirror = sections - section

    def fetched(source, target, slot):
        return [pltpu.make_async_copy(
            source.at[0, pl.ds(3 * a, 3)], target.at[pl.ds(3 * a, 3)], weight_sem.at[slot, a])
            for a in range(3)]

    first_weights = fetched(conv_first, first_w, 0)
    second_weights = fetched(conv_second, second_w, 1)
    skip_weights = fetched(conv_skip, skip_w, 2)
    biases = [
        pltpu.make_async_copy(bias_first, first_b, weight_sem.at[3, 0]),
        pltpu.make_async_copy(bias_second, second_b, weight_sem.at[3, 1]),
    ]
    own_rows = pltpu.make_async_copy(images, land.at[:, pl.ds(HALO, rows)], image_sem)

    even = lax.rem(strip, 2) == 0
    inner = jnp.where(even, strip + 1, strip - 1)
    outer = jnp.where(even, strip - 1, strip + 1)
    has_inner = inner < strips
    has_outer = jnp.where(even, has_above, has_below)
    half = rows // 2
    inner_row = jnp.where(even, rows - half, 0)
    outer_row = jnp.where(even, 0, rows - half)
    inner_edge = jnp.where(even, rows - HALO, 0)
    outer_edge = jnp.where(even, 0, rows - HALO)
    inner_halo = jnp.where(even, 0, HALO + rows)
    outer_halo = jnp.where(even, HALO + rows, 0)

    landed = land.at[:, pl.ds(HALO, rows)]

    def halves(m):
        return [pltpu.make_async_remote_copy(
            src_ref=result.at[m, pl.ds(row, half)], dst_ref=land.at[m, pl.ds(HALO + row, half)],
            send_sem=land_send.at[m, part], recv_sem=land_recv.at[m, part],
            device_id=(section + 1, strip), device_id_type=MESH)
            for part, row in enumerate((inner_row, outer_row))]

    def edge(m, source, to_section, part):
        send = edge_send if source is result else own_send
        row, halo, to_strip = ((inner_edge, inner_halo, inner), (outer_edge, outer_halo, outer))[part]
        return pltpu.make_async_remote_copy(
            src_ref=source.at[m, pl.ds(row, HALO)], dst_ref=land.at[m, pl.ds(halo, HALO)],
            send_sem=send.at[m, part], recv_sem=edge_recv.at[m, part],
            device_id=(to_section, to_strip), device_id_type=MESH)

    def start_outer(m, source, to_section):
        @pl.when(has_outer)
        def _():
            edge(m, source, to_section, 1).start()

    def start_inner(m):
        @pl.when(has_inner)
        def _():
            edge(m, landed, section, 0).start()

    def sent_outer(m, source):
        @pl.when(has_outer)
        def _():
            edge(m, source, section, 1).wait_send()

    def sent_inner(m):
        @pl.when(has_inner)
        def _():
            edge(m, landed, section, 0).wait_send()

    def skip_edge(m, part):
        row, halo, to_strip = ((inner_edge, inner_halo, inner), (outer_edge, outer_halo, outer))[part]
        return pltpu.make_async_remote_copy(
            src_ref=skip_land.at[m, pl.ds(HALO + row, HALO)], dst_ref=skip_land.at[m, pl.ds(halo, HALO)],
            send_sem=skip_edge_send.at[m, part], recv_sem=skip_edge_recv.at[m, part],
            device_id=(section, to_strip), device_id_type=MESH)

    beside = ((has_inner, 0), (has_outer, 1))

    def written(m):
        return [pltpu.make_async_copy(
            result.at[m, pl.ds(row, half)], out.at[0, m, pl.ds(row, half)], out_sem.at[m, part])
            for part, row in enumerate((inner_row, outer_row))]

    def skipped(m):
        return pltpu.make_async_remote_copy(
            src_ref=land.at[m, pl.ds(HALO, rows)], dst_ref=skip_land.at[m, pl.ds(HALO, rows)],
            send_sem=skip_send.at[m], recv_sem=skip_recv.at[m],
            device_id=(mirror, strip), device_id_type=MESH)

    pl.when(is_first)(own_rows.start)
    for copy in first_weights + biases + second_weights:
        copy.start()

    @pl.when(section >= middle)
    def _():
        for copy in skip_weights:
            copy.start()

    barrier = pltpu.get_barrier_semaphore()

    def greet(condition, to_section, to_strip):
        @pl.when(condition)
        def _():
            pl.semaphore_signal(barrier, inc=1, device_id=(to_section, to_strip), device_id_type=MESH)

    greet(has_inner, section, inner)
    greet(has_outer, jnp.where(is_first, section, section - 1), outer)
    greet(section > 0, section - 1, strip)
    greet(takes_skip, mirror, strip)
    greet(takes_skip & has_outer, section, outer)
    inner_count, outer_count = has_inner.astype(jnp.int32), has_outer.astype(jnp.int32)
    expected = (
        inner_count
        + jnp.where(is_first | takes_skip, outer_count, 0)
        + jnp.where(has_next, outer_count + 1, 0)
        + jnp.where(sends_skip, 1, 0)
    )

    @pl.when(expected > 0)
    def _():
        pl.semaphore_wait(barrier, expected)

    @pl.when(is_first)
    def _():
        own_rows.wait()
        for m in range(micro):
            start_outer(m, landed, section)
        for m in range(micro):
            start_inner(m)

    blank = jnp.zeros((micro, HALO, cols, channels), land.dtype)

    @pl.when(jnp.logical_not(has_above))
    def _():
        land[:, 0:HALO] = blank
        skip_land[:, 0:HALO] = blank

    @pl.when(jnp.logical_not(has_below))
    def _():
        land[:, HALO + rows:] = blank
        skip_land[:, HALO + rows:] = blank

    for copy in first_weights + biases:
        copy.wait()

    @pl.when(section >= middle)
    def _():
        for copy in skip_weights:
            copy.wait()

    @pl.when(section == middle)
    def _():
        def add(tap, carry):
            total = first_w[tap].astype(jnp.float32) + skip_w[tap].astype(jnp.float32)
            first_w[tap] = total.astype(first_w.dtype)
            return carry
        lax.fori_loop(0, 9, add, 0)

    def convolve(window, weight, out_rows):
        size = out_rows * cols
        shape = (out_rows, cols, channels)
        read = jnp.concatenate([window(a).reshape(size, channels) for a in range(3)], axis=1)
        column = lax.broadcasted_iota(jnp.int32, shape, 1)

        def product(b):
            taps = jnp.concatenate([weight[3 * a + b] for a in range(3)], axis=0)
            return jnp.dot(read, taps, preferred_element_type=jnp.float32)

        def moved(value, distance, edge_column):
            rolled = pltpu.roll(value, distance % size, axis=0).reshape(shape)
            return jnp.where(column == edge_column, 0.0, rolled)

        left = moved(product(0), 1, 0)
        right = moved(product(2), -1, cols - 1)
        return left + right + product(1).reshape(shape)

    hidden_rows = rows + 2
    first_bias = first_b[...].reshape(1, 1, channels)
    second_bias = second_b[...].reshape(1, 1, channels)

    @pl.when(takes_skip)
    def _():
        for m in range(micro):
            skipped(m).wait_recv()
            for condition, part in beside:
                pl.when(condition)(skip_edge(m, part).start)

        def skip_step(m, carry):
            for condition, part in beside:
                pl.when(condition)(skip_edge(m, part).wait_recv)
            pre[m] = first_bias + convolve(
                lambda a: skip_land[m, pl.ds(a, hidden_rows)], skip_w, hidden_rows)
            return carry

        lax.fori_loop(0, micro, skip_step, 0)

    @pl.when(jnp.logical_not(takes_skip))
    def _():
        pre[...] = jnp.broadcast_to(first_bias, pre.shape)


    def hide(m, begin, count):
        hidden = convolve(lambda a: land[m, pl.ds(begin + a, count)], first_w, count)
        hidden = jnp.maximum(hidden + pre[m, pl.ds(begin, count)], 0.0)
        row = begin + lax.broadcasted_iota(jnp.int32, hidden.shape, 0)
        least = jnp.where(has_above, 0, 1)
        most = jnp.where(has_below, hidden_rows, hidden_rows - 1)
        hidden = jnp.where((row >= least) & (row < most), hidden, 0.0)
        hidden_map[pl.ds(begin, count)] = hidden.astype(jnp.bfloat16)

    def finish(m, begin):
        final = convolve(lambda a: hidden_map[pl.ds(begin + a, half)], second_w, half)
        result[m, pl.ds(begin, half)] = jnp.maximum(final + second_bias, 0.0).astype(jnp.bfloat16)

    def step(m, carry):
        @pl.when(section > 0)
        def _():
            inner_half, outer_half = halves(m)
            inner_half.wait_recv()
            start_inner(m)
            outer_half.wait_recv()

        @pl.when(sends_skip)
        def _():
            skipped(m).start()

        @pl.when(has_inner)
        def _():
            edge(m, result, section, 0).wait_recv()

        inner_half, outer_half = halves(m)
        hide(m, jnp.where(even, HALO, 0), rows)

        @pl.when(m == 0)
        def _():
            for copy in second_weights:
                copy.wait()

        finish(m, inner_row)
        pl.when(has_next)(inner_half.start)
        written(m)[0].start()

        @pl.when(has_outer)
        def _():
            edge(m, result, section, 1).wait_recv()

        hide(m, jnp.where(even, 0, rows), HALO)
        finish(m, outer_row)

        @pl.when(has_next)
        def _():
            start_outer(m, result, section + 1)
            outer_half.start()

        written(m)[1].start()
        return carry

    lax.fori_loop(0, micro, step, 0)

    for m in range(micro):
        for copy in written(m):
            copy.wait()

        sent_inner(m)

        @pl.when(takes_skip)
        def _():
            for condition, part in beside:
                pl.when(condition)(skip_edge(m, part).wait_send)

        @pl.when(is_first)
        def _():
            sent_outer(m, landed)

        @pl.when(has_next)
        def _():
            for copy in halves(m):
                copy.wait_send()
            sent_outer(m, result)

        @pl.when(sends_skip)
        def _():
            skipped(m).wait_send()


def body(images, conv_first, conv_skip, conv_second, bias_first, bias_second):
    sections = lax.axis_size("section")
    strips = lax.axis_size("strip")
    arguments = (images, conv_first, conv_skip, conv_second, bias_first, bias_second)
    micro, rows, cols, channels = images.shape
    padded = (micro, rows + 2 * HALO, cols, channels)
    weight = conv_first.shape[1:]
    copies = pltpu.SemaphoreType.DMA((micro, 2))
    pixels = rows * cols
    flops = 2 * micro * 2 * pixels * channels * channels * 9
    return pl.pallas_call(
        functools.partial(kernel, sections, strips),
        out_shape=jax.ShapeDtypeStruct((1, micro, rows, cols, channels), jnp.bfloat16),
        in_specs=[pl.BlockSpec(memory_space=pltpu.HBM)] * 6,
        out_specs=pl.BlockSpec(memory_space=pltpu.HBM),
        scratch_shapes=[
            pltpu.VMEM(weight, jnp.bfloat16),
            pltpu.VMEM(weight, jnp.bfloat16),
            pltpu.VMEM(weight, jnp.bfloat16),
            pltpu.VMEM((1, channels), jnp.float32),
            pltpu.VMEM((1, channels), jnp.float32),
            pltpu.VMEM(padded, jnp.bfloat16),
            pltpu.VMEM(padded, jnp.bfloat16),
            pltpu.VMEM((micro, rows, cols, channels), jnp.bfloat16),
            pltpu.VMEM((rows + 2, cols, channels), jnp.bfloat16),
            pltpu.VMEM((micro, rows + 2, cols, channels), jnp.float32),
            pltpu.SemaphoreType.DMA((4, 3)),
            pltpu.SemaphoreType.DMA,
            copies, copies, copies, copies, copies, copies, copies,
            pltpu.SemaphoreType.DMA((micro,)),
            pltpu.SemaphoreType.DMA((micro,)),
            copies,
        ],
        compiler_params=pltpu.CompilerParams(
            collective_id=0, has_side_effects=True, vmem_limit_bytes=32 * 1024 * 1024
        ),
        cost_estimate=pl.CostEstimate(
            flops=flops, bytes_accessed=3 * conv_first.size * 2, transcendentals=0
        ),
    )(*[pltpu.with_memory_space_constraint(value, pltpu.HBM) for value in arguments])


def solution(mesh):
    placed = (
        P(None, "strip", None, None),
        P("section", None, None, None),
        P("section", None, None, None),
        P("section", None, None, None),
        P("section", None),
        P("section", None),
    )
    return jax.shard_map(
        body,
        mesh=mesh,
        in_specs=placed,
        out_specs=P("section", None, "strip", None, None),
        check_vma=False,
    )
```

```python
import functools

import jax
import jax.numpy as jnp
from jax import lax
from jax.experimental import pallas as pl
from jax.experimental.pallas import tpu as pltpu
from jax.sharding import PartitionSpec as P

MESH = pl.DeviceIdType.MESH
HALO = 2


def kernel(
    sections, strips,
    images, conv_first, conv_skip, conv_second, bias_first, bias_second,
    out,
    first_w, skip_w, second_w, first_b, second_b,
    land, skip_land, hidden_map, pre,
    weight_sem, image_sem, own_send, edge_send, edge_recv, skip_edge_send, skip_edge_recv, land_send, land_recv, skip_send, skip_recv,
):
    section = lax.axis_index("section")
    strip = lax.axis_index("strip")
    result = out.at[0]
    micro, rows, cols, channels = images.shape
    middle = sections // 2
    is_first = section == 0
    has_next = section + 1 < sections
    has_above = strip > 0
    has_below = strip + 1 < strips
    sends_skip = (section > 0) & (section < middle)
    takes_skip = section > middle
    mirror = sections - section

    weights = (
        pltpu.make_async_copy(conv_first.at[0], first_w, weight_sem.at[0]),
        pltpu.make_async_copy(conv_second.at[0], second_w, weight_sem.at[1]),
        pltpu.make_async_copy(bias_first, first_b, weight_sem.at[2]),
        pltpu.make_async_copy(bias_second, second_b, weight_sem.at[3]),
    )
    skip_weight = pltpu.make_async_copy(conv_skip.at[0], skip_w, weight_sem.at[4])
    own_rows = pltpu.make_async_copy(images, land.at[:, pl.ds(HALO, rows)], image_sem)

    even = lax.rem(strip, 2) == 0
    inner = jnp.where(even, strip + 1, strip - 1)
    outer = jnp.where(even, strip - 1, strip + 1)
    has_inner = inner < strips
    has_outer = jnp.where(even, has_above, has_below)
    half = rows // 2
    inner_row = jnp.where(even, rows - half, 0)
    outer_row = jnp.where(even, 0, rows - half)
    inner_edge = jnp.where(even, rows - HALO, 0)
    outer_edge = jnp.where(even, 0, rows - HALO)
    inner_halo = jnp.where(even, 0, HALO + rows)
    outer_halo = jnp.where(even, HALO + rows, 0)

    landed = land.at[:, pl.ds(HALO, rows)]

    def halves(m):
        return [pltpu.make_async_remote_copy(
            src_ref=result.at[m, pl.ds(row, half)], dst_ref=land.at[m, pl.ds(HALO + row, half)],
            send_sem=land_send.at[m, part], recv_sem=land_recv.at[m, part],
            device_id=(section + 1, strip), device_id_type=MESH)
            for part, row in enumerate((inner_row, outer_row))]

    def edge(m, source, to_section, part):
        send = edge_send if source is result else own_send
        row, halo, to_strip = ((inner_edge, inner_halo, inner), (outer_edge, outer_halo, outer))[part]
        return pltpu.make_async_remote_copy(
            src_ref=source.at[m, pl.ds(row, HALO)], dst_ref=land.at[m, pl.ds(halo, HALO)],
            send_sem=send.at[m, part], recv_sem=edge_recv.at[m, part],
            device_id=(to_section, to_strip), device_id_type=MESH)

    def start_outer(m, source, to_section):
        @pl.when(has_outer)
        def _():
            edge(m, source, to_section, 1).start()

    def start_inner(m):
        @pl.when(has_inner)
        def _():
            edge(m, landed, section, 0).start()

    def sent_outer(m, source):
        @pl.when(has_outer)
        def _():
            edge(m, source, section, 1).wait_send()

    def sent_inner(m):
        @pl.when(has_inner)
        def _():
            edge(m, landed, section, 0).wait_send()

    def skip_edge(m, part):
        row, halo, to_strip = ((inner_edge, inner_halo, inner), (outer_edge, outer_halo, outer))[part]
        return pltpu.make_async_remote_copy(
            src_ref=skip_land.at[m, pl.ds(HALO + row, HALO)], dst_ref=skip_land.at[m, pl.ds(halo, HALO)],
            send_sem=skip_edge_send.at[m, part], recv_sem=skip_edge_recv.at[m, part],
            device_id=(section, to_strip), device_id_type=MESH)

    beside = ((has_inner, 0), (has_outer, 1))

    def skipped(m):
        return pltpu.make_async_remote_copy(
            src_ref=land.at[m, pl.ds(HALO, rows)], dst_ref=skip_land.at[m, pl.ds(HALO, rows)],
            send_sem=skip_send.at[m], recv_sem=skip_recv.at[m],
            device_id=(mirror, strip), device_id_type=MESH)

    pl.when(is_first)(own_rows.start)
    for copy in weights:
        copy.start()
    pl.when(section >= middle)(skip_weight.start)

    barrier = pltpu.get_barrier_semaphore()

    def greet(condition, to_section, to_strip):
        @pl.when(condition)
        def _():
            pl.semaphore_signal(barrier, inc=1, device_id=(to_section, to_strip), device_id_type=MESH)

    greet(has_inner, section, inner)
    greet(has_outer, jnp.where(is_first, section, section - 1), outer)
    greet(section > 0, section - 1, strip)
    greet(takes_skip, mirror, strip)
    greet(takes_skip & has_outer, section, outer)
    inner_count, outer_count = has_inner.astype(jnp.int32), has_outer.astype(jnp.int32)
    expected = (
        inner_count
        + jnp.where(is_first | takes_skip, outer_count, 0)
        + jnp.where(has_next, outer_count + 1, 0)
        + jnp.where(sends_skip, 1, 0)
    )

    @pl.when(expected > 0)
    def _():
        pl.semaphore_wait(barrier, expected)

    @pl.when(is_first)
    def _():
        own_rows.wait()
        for m in range(micro):
            start_outer(m, landed, section)
        for m in range(micro):
            start_inner(m)

    blank = jnp.zeros((micro, HALO, cols, channels), land.dtype)

    @pl.when(jnp.logical_not(has_above))
    def _():
        land[:, 0:HALO] = blank
        skip_land[:, 0:HALO] = blank

    @pl.when(jnp.logical_not(has_below))
    def _():
        land[:, HALO + rows:] = blank
        skip_land[:, HALO + rows:] = blank

    pl.when(section >= middle)(skip_weight.wait)
    for copy in weights:
        copy.wait()

    @pl.when(section == middle)
    def _():
        def add(tap, carry):
            total = first_w[tap].astype(jnp.float32) + skip_w[tap].astype(jnp.float32)
            first_w[tap] = total.astype(first_w.dtype)
            return carry
        lax.fori_loop(0, 9, add, 0)

    def convolve(window, weight, out_rows):
        size = out_rows * cols
        shape = (out_rows, cols, channels)
        read = jnp.concatenate([window(a).reshape(size, channels) for a in range(3)], axis=1)
        column = lax.broadcasted_iota(jnp.int32, shape, 1)

        def product(b):
            taps = jnp.concatenate([weight[3 * a + b] for a in range(3)], axis=0)
            return jnp.dot(read, taps, preferred_element_type=jnp.float32)

        def moved(value, distance, edge_column):
            rolled = pltpu.roll(value, distance % size, axis=0).reshape(shape)
            return jnp.where(column == edge_column, 0.0, rolled)

        left = moved(product(0), 1, 0)
        right = moved(product(2), -1, cols - 1)
        return left + right + product(1).reshape(shape)

    hidden_rows = rows + 2
    first_bias = first_b[...].reshape(1, 1, channels)
    second_bias = second_b[...].reshape(1, 1, channels)

    @pl.when(takes_skip)
    def _():
        for m in range(micro):
            skipped(m).wait_recv()
            for condition, part in beside:
                pl.when(condition)(skip_edge(m, part).start)

        def skip_step(m, carry):
            for condition, part in beside:
                pl.when(condition)(skip_edge(m, part).wait_recv)
            pre[m] = first_bias + convolve(
                lambda a: skip_land[m, pl.ds(a, hidden_rows)], skip_w, hidden_rows)
            return carry

        lax.fori_loop(0, micro, skip_step, 0)

    @pl.when(jnp.logical_not(takes_skip))
    def _():
        pre[...] = jnp.broadcast_to(first_bias, pre.shape)


    def hide(m, begin, count):
        hidden = convolve(lambda a: land[m, pl.ds(begin + a, count)], first_w, count)
        hidden = jnp.maximum(hidden + pre[m, pl.ds(begin, count)], 0.0)
        row = begin + lax.broadcasted_iota(jnp.int32, hidden.shape, 0)
        least = jnp.where(has_above, 0, 1)
        most = jnp.where(has_below, hidden_rows, hidden_rows - 1)
        hidden = jnp.where((row >= least) & (row < most), hidden, 0.0)
        hidden_map[pl.ds(begin, count)] = hidden.astype(jnp.bfloat16)

    def finish(m, begin):
        final = convolve(lambda a: hidden_map[pl.ds(begin + a, half)], second_w, half)
        result[m, pl.ds(begin, half)] = jnp.maximum(final + second_bias, 0.0).astype(jnp.bfloat16)

    def step(m, carry):
        @pl.when(section > 0)
        def _():
            inner_half, outer_half = halves(m)
            inner_half.wait_recv()
            start_inner(m)
            outer_half.wait_recv()

        @pl.when(sends_skip)
        def _():
            skipped(m).start()

        @pl.when(has_inner)
        def _():
            edge(m, result, section, 0).wait_recv()

        inner_half, outer_half = halves(m)
        hide(m, jnp.where(even, HALO, 0), rows)
        finish(m, inner_row)
        pl.when(has_next)(inner_half.start)

        @pl.when(has_outer)
        def _():
            edge(m, result, section, 1).wait_recv()

        hide(m, jnp.where(even, 0, rows), HALO)
        finish(m, outer_row)

        @pl.when(has_next)
        def _():
            start_outer(m, result, section + 1)
            outer_half.start()

        return carry

    lax.fori_loop(0, micro, step, 0)

    for m in range(micro):
        sent_inner(m)

        @pl.when(takes_skip)
        def _():
            for condition, part in beside:
                pl.when(condition)(skip_edge(m, part).wait_send)

        @pl.when(is_first)
        def _():
            sent_outer(m, landed)

        @pl.when(has_next)
        def _():
            for copy in halves(m):
                copy.wait_send()
            sent_outer(m, result)

        @pl.when(sends_skip)
        def _():
            skipped(m).wait_send()


def body(images, conv_first, conv_skip, conv_second, bias_first, bias_second):
    sections = lax.axis_size("section")
    strips = lax.axis_size("strip")
    arguments = (images, conv_first, conv_skip, conv_second, bias_first, bias_second)
    micro, rows, cols, channels = images.shape
    padded = (micro, rows + 2 * HALO, cols, channels)
    weight = conv_first.shape[1:]
    copies = pltpu.SemaphoreType.DMA((micro, 2))
    pixels = rows * cols
    flops = 2 * micro * 2 * pixels * channels * channels * 9
    return pl.pallas_call(
        functools.partial(kernel, sections, strips),
        out_shape=jax.ShapeDtypeStruct((1, micro, rows, cols, channels), jnp.bfloat16),
        in_specs=[pl.BlockSpec(memory_space=pltpu.HBM)] * 6,
        out_specs=pl.BlockSpec(memory_space=pltpu.VMEM),
        scratch_shapes=[
            pltpu.VMEM(weight, jnp.bfloat16),
            pltpu.VMEM(weight, jnp.bfloat16),
            pltpu.VMEM(weight, jnp.bfloat16),
            pltpu.VMEM((1, channels), jnp.float32),
            pltpu.VMEM((1, channels), jnp.float32),
            pltpu.VMEM(padded, jnp.bfloat16),
            pltpu.VMEM(padded, jnp.bfloat16),
            pltpu.VMEM((rows + 2, cols, channels), jnp.bfloat16),
            pltpu.VMEM((micro, rows + 2, cols, channels), jnp.float32),
            pltpu.SemaphoreType.DMA((5,)),
            pltpu.SemaphoreType.DMA,
            copies, copies, copies, copies, copies, copies, copies,
            pltpu.SemaphoreType.DMA((micro,)),
            pltpu.SemaphoreType.DMA((micro,)),
        ],
        compiler_params=pltpu.CompilerParams(
            collective_id=0, has_side_effects=True, vmem_limit_bytes=32 * 1024 * 1024
        ),
        cost_estimate=pl.CostEstimate(
            flops=flops, bytes_accessed=3 * conv_first.size * 2, transcendentals=0
        ),
    )(*[pltpu.with_memory_space_constraint(value, pltpu.HBM) for value in arguments])


def solution(mesh):
    placed = (
        P(None, "strip", None, None),
        P("section", None, None, None),
        P("section", None, None, None),
        P("section", None, None, None),
        P("section", None),
        P("section", None),
    )
    return jax.shard_map(
        body,
        mesh=mesh,
        in_specs=placed,
        out_specs=P("section", None, "strip", None, None),
        check_vma=False,
    )
```

```python
import functools

import jax
import jax.numpy as jnp
from jax import lax
from jax.experimental import pallas as pl
from jax.experimental.pallas import tpu as pltpu
from jax.sharding import PartitionSpec as P

MESH = pl.DeviceIdType.MESH
HALO = 2


def kernel(
    sections, strips,
    images, conv_first, conv_skip, conv_second, bias_first, bias_second,
    out,
    first_w, skip_w, second_w, first_b, second_b,
    land, skip_land, hidden_map, pre,
    weight_sem, image_sem, own_send, edge_send, edge_recv, skip_edge_send, skip_edge_recv, land_send, land_recv, skip_send, skip_recv,
):
    section = lax.axis_index("section")
    strip = lax.axis_index("strip")
    result = out.at[0]
    micro, rows, cols, channels = images.shape
    middle = sections // 2
    is_first = section == 0
    has_next = section + 1 < sections
    has_above = strip > 0
    has_below = strip + 1 < strips
    sends_skip = (section > 0) & (section < middle)
    takes_skip = section > middle
    mirror = sections - section

    weights = (
        pltpu.make_async_copy(conv_first.at[0], first_w, weight_sem.at[0]),
        pltpu.make_async_copy(conv_second.at[0], second_w, weight_sem.at[1]),
        pltpu.make_async_copy(bias_first, first_b, weight_sem.at[2]),
        pltpu.make_async_copy(bias_second, second_b, weight_sem.at[3]),
    )
    skip_weight = pltpu.make_async_copy(conv_skip.at[0], skip_w, weight_sem.at[4])
    own_rows = pltpu.make_async_copy(images, land.at[:, pl.ds(HALO, rows)], image_sem)

    even = lax.rem(strip, 2) == 0
    inner = jnp.where(even, strip + 1, strip - 1)
    outer = jnp.where(even, strip - 1, strip + 1)
    has_inner = inner < strips
    has_outer = jnp.where(even, has_above, has_below)
    half = rows // 2
    inner_row = jnp.where(even, rows - half, 0)
    outer_row = jnp.where(even, 0, rows - half)
    inner_edge = jnp.where(even, rows - HALO, 0)
    outer_edge = jnp.where(even, 0, rows - HALO)
    inner_halo = jnp.where(even, 0, HALO + rows)
    outer_halo = jnp.where(even, HALO + rows, 0)

    landed = land.at[:, pl.ds(HALO, rows)]

    def halves(m):
        return [pltpu.make_async_remote_copy(
            src_ref=result.at[m, pl.ds(row, half)], dst_ref=land.at[m, pl.ds(HALO + row, half)],
            send_sem=land_send.at[m, part], recv_sem=land_recv.at[m, part],
            device_id=(section + 1, strip), device_id_type=MESH)
            for part, row in enumerate((inner_row, outer_row))]

    def edge(m, source, to_section, part):
        send = edge_send if source is result else own_send
        row, halo, to_strip = ((inner_edge, inner_halo, inner), (outer_edge, outer_halo, outer))[part]
        return pltpu.make_async_remote_copy(
            src_ref=source.at[m, pl.ds(row, HALO)], dst_ref=land.at[m, pl.ds(halo, HALO)],
            send_sem=send.at[m, part], recv_sem=edge_recv.at[m, part],
            device_id=(to_section, to_strip), device_id_type=MESH)

    def start_outer(m, source, to_section):
        @pl.when(has_outer)
        def _():
            edge(m, source, to_section, 1).start()

    def start_inner(m):
        @pl.when(has_inner)
        def _():
            edge(m, landed, section, 0).start()

    def sent_outer(m, source):
        @pl.when(has_outer)
        def _():
            edge(m, source, section, 1).wait_send()

    def sent_inner(m):
        @pl.when(has_inner)
        def _():
            edge(m, landed, section, 0).wait_send()

    def skip_edge(m, part):
        row, halo, to_strip = ((inner_edge, inner_halo, inner), (outer_edge, outer_halo, outer))[part]
        return pltpu.make_async_remote_copy(
            src_ref=skip_land.at[m, pl.ds(HALO + row, HALO)], dst_ref=skip_land.at[m, pl.ds(halo, HALO)],
            send_sem=skip_edge_send.at[m, part], recv_sem=skip_edge_recv.at[m, part],
            device_id=(section, to_strip), device_id_type=MESH)

    beside = ((has_inner, 0), (has_outer, 1))

    def skipped(m):
        return pltpu.make_async_remote_copy(
            src_ref=land.at[m, pl.ds(HALO, rows)], dst_ref=skip_land.at[m, pl.ds(HALO, rows)],
            send_sem=skip_send.at[m], recv_sem=skip_recv.at[m],
            device_id=(mirror, strip), device_id_type=MESH)

    pl.when(is_first)(own_rows.start)
    for copy in weights:
        copy.start()
    pl.when(section >= middle)(skip_weight.start)

    barrier = pltpu.get_barrier_semaphore()

    def greet(condition, to_section, to_strip):
        @pl.when(condition)
        def _():
            pl.semaphore_signal(barrier, inc=1, device_id=(to_section, to_strip), device_id_type=MESH)

    greet(has_inner, section, inner)
    greet(has_outer, jnp.where(is_first, section, section - 1), outer)
    greet(section > 0, section - 1, strip)
    greet(takes_skip, mirror, strip)
    greet(takes_skip & has_outer, section, outer)
    inner_count, outer_count = has_inner.astype(jnp.int32), has_outer.astype(jnp.int32)
    expected = (
        inner_count
        + jnp.where(is_first | takes_skip, outer_count, 0)
        + jnp.where(has_next, outer_count + 1, 0)
        + jnp.where(sends_skip, 1, 0)
    )

    @pl.when(expected > 0)
    def _():
        pl.semaphore_wait(barrier, expected)

    @pl.when(is_first)
    def _():
        own_rows.wait()
        for m in range(micro):
            start_outer(m, landed, section)
        for m in range(micro):
            start_inner(m)

    blank = jnp.zeros((micro, HALO, cols, channels), land.dtype)

    @pl.when(jnp.logical_not(has_above))
    def _():
        land[:, 0:HALO] = blank
        skip_land[:, 0:HALO] = blank

    @pl.when(jnp.logical_not(has_below))
    def _():
        land[:, HALO + rows:] = blank
        skip_land[:, HALO + rows:] = blank

    pl.when(section >= middle)(skip_weight.wait)
    for copy in weights:
        copy.wait()

    @pl.when(section == middle)
    def _():
        def add(tap, carry):
            total = first_w[tap].astype(jnp.float32) + skip_w[tap].astype(jnp.float32)
            first_w[tap] = total.astype(first_w.dtype)
            return carry
        lax.fori_loop(0, 9, add, 0)

    def convolve(window, weight, out_rows):
        size = out_rows * cols
        shape = (out_rows, cols, channels)
        read = jnp.concatenate([window(a).reshape(size, channels) for a in range(3)], axis=1)
        column = lax.broadcasted_iota(jnp.int32, shape, 1)

        def product(b):
            taps = jnp.concatenate([weight[3 * a + b] for a in range(3)], axis=0)
            return jnp.dot(read, taps, preferred_element_type=jnp.float32)

        def moved(value, distance, edge_column):
            rolled = pltpu.roll(value, distance % size, axis=0).reshape(shape)
            return jnp.where(column == edge_column, 0.0, rolled)

        left = moved(product(0), 1, 0)
        right = moved(product(2), -1, cols - 1)
        return left + right + product(1).reshape(shape)

    hidden_rows = rows + 2
    first_bias = first_b[...].reshape(1, 1, channels)
    second_bias = second_b[...].reshape(1, 1, channels)

    @pl.when(takes_skip)
    def _():
        for m in range(micro):
            skipped(m).wait_recv()
            for condition, part in beside:
                pl.when(condition)(skip_edge(m, part).start)

        def skip_step(m, carry):
            for condition, part in beside:
                pl.when(condition)(skip_edge(m, part).wait_recv)
            pre[m] = first_bias + convolve(
                lambda a: skip_land[m, pl.ds(a, hidden_rows)], skip_w, hidden_rows)
            return carry

        lax.fori_loop(0, micro, skip_step, 0)

    @pl.when(jnp.logical_not(takes_skip))
    def _():
        pre[...] = jnp.broadcast_to(first_bias, pre.shape)


    def hide(m, begin, count):
        hidden = convolve(lambda a: land[m, pl.ds(begin + a, count)], first_w, count)
        hidden = jnp.maximum(hidden + pre[m, pl.ds(begin, count)], 0.0)
        row = begin + lax.broadcasted_iota(jnp.int32, hidden.shape, 0)
        least = jnp.where(has_above, 0, 1)
        most = jnp.where(has_below, hidden_rows, hidden_rows - 1)
        hidden = jnp.where((row >= least) & (row < most), hidden, 0.0)
        hidden_map[pl.ds(begin, count)] = hidden.astype(jnp.bfloat16)

    def finish(m, begin):
        final = convolve(lambda a: hidden_map[pl.ds(begin + a, half)], second_w, half)
        result[m, pl.ds(begin, half)] = jnp.maximum(final + second_bias, 0.0).astype(jnp.bfloat16)

    def step(m, carry):
        @pl.when(section > 0)
        def _():
            inner_half, outer_half = halves(m)
            inner_half.wait_recv()
            start_inner(m)
            outer_half.wait_recv()

        @pl.when(has_inner)
        def _():
            edge(m, result, section, 0).wait_recv()

        inner_half, outer_half = halves(m)
        hide(m, jnp.where(even, HALO, 0), rows)
        finish(m, inner_row)
        pl.when(has_next)(inner_half.start)
        pl.when(sends_skip)(skipped(m).start)

        @pl.when(has_outer)
        def _():
            edge(m, result, section, 1).wait_recv()

        hide(m, jnp.where(even, 0, rows), HALO)
        finish(m, outer_row)

        @pl.when(has_next)
        def _():
            start_outer(m, result, section + 1)
            outer_half.start()

        return carry

    lax.fori_loop(0, micro, step, 0)

    for m in range(micro):
        sent_inner(m)

        @pl.when(takes_skip)
        def _():
            for condition, part in beside:
                pl.when(condition)(skip_edge(m, part).wait_send)

        @pl.when(is_first)
        def _():
            sent_outer(m, landed)

        @pl.when(has_next)
        def _():
            for copy in halves(m):
                copy.wait_send()
            sent_outer(m, result)

        @pl.when(sends_skip)
        def _():
            skipped(m).wait_send()


def body(images, conv_first, conv_skip, conv_second, bias_first, bias_second):
    sections = lax.axis_size("section")
    strips = lax.axis_size("strip")
    arguments = (images, conv_first, conv_skip, conv_second, bias_first, bias_second)
    micro, rows, cols, channels = images.shape
    padded = (micro, rows + 2 * HALO, cols, channels)
    weight = conv_first.shape[1:]
    copies = pltpu.SemaphoreType.DMA((micro, 2))
    pixels = rows * cols
    flops = 2 * micro * 2 * pixels * channels * channels * 9
    return pl.pallas_call(
        functools.partial(kernel, sections, strips),
        out_shape=jax.ShapeDtypeStruct((1, micro, rows, cols, channels), jnp.bfloat16),
        in_specs=[pl.BlockSpec(memory_space=pltpu.HBM)] * 6,
        out_specs=pl.BlockSpec(memory_space=pltpu.VMEM),
        scratch_shapes=[
            pltpu.VMEM(weight, jnp.bfloat16),
            pltpu.VMEM(weight, jnp.bfloat16),
            pltpu.VMEM(weight, jnp.bfloat16),
            pltpu.VMEM((1, channels), jnp.float32),
            pltpu.VMEM((1, channels), jnp.float32),
            pltpu.VMEM(padded, jnp.bfloat16),
            pltpu.VMEM(padded, jnp.bfloat16),
            pltpu.VMEM((rows + 2, cols, channels), jnp.bfloat16),
            pltpu.VMEM((micro, rows + 2, cols, channels), jnp.float32),
            pltpu.SemaphoreType.DMA((5,)),
            pltpu.SemaphoreType.DMA,
            copies, copies, copies, copies, copies, copies, copies,
            pltpu.SemaphoreType.DMA((micro,)),
            pltpu.SemaphoreType.DMA((micro,)),
        ],
        compiler_params=pltpu.CompilerParams(
            collective_id=0, has_side_effects=True, vmem_limit_bytes=32 * 1024 * 1024
        ),
        cost_estimate=pl.CostEstimate(
            flops=flops, bytes_accessed=3 * conv_first.size * 2, transcendentals=0
        ),
    )(*[pltpu.with_memory_space_constraint(value, pltpu.HBM) for value in arguments])


def solution(mesh):
    placed = (
        P(None, "strip", None, None),
        P("section", None, None, None),
        P("section", None, None, None),
        P("section", None, None, None),
        P("section", None),
        P("section", None),
    )
    return jax.shard_map(
        body,
        mesh=mesh,
        in_specs=placed,
        out_specs=P("section", None, "strip", None, None),
        check_vma=False,
    )
```
